32 devices in a mesh: sens: 4 (over y, core), par: 8 (over z, x).
Axes of the slice: x: 2, y: 2, z: 4, core: 2. Of those that a mesh axis runs over, the one named last changes fastest.
Arguments:
- data: bfloat16 [32, 600, 420], P(None, 'sens'), may hold values from -6 to 6
- green: bfloat16 [64, 600, 2, 1024], P(None, 'sens', None, 'par'), may hold values from -0.1875 to 0.1875
- freqs: int32 [64], replicated, may hold values from 1 to 209, as said below
- sensor_order: int32 [600], P('sens'), may hold values from 0 to 599, each once
- kappa: float32 [8, 128], P('par'), may hold values from 0.05 to 0.5
- theta: float32 [8, 128], P('par'), may hold values from 0.5 to 2
Outputs:
- prior_field: bfloat16 [32, 420, 8, 128], P('sens', None, 'par')
The draws below stay inside these ranges and needn't reach their ends.
Inputs may be any that keep to these rules, and one draw needn't show every extreme that they name: `freqs`: distinct; both 1 and 209 appear. `sensor_order`: each sensor fills exactly one slot.
All inputs are finite; a program needn't handle non-finite values.
Results may differ from the reference program's by a relative error of at most 0.015.
Values may be sent and summed in bfloat16 or wider, within the bound.
A program may use at most 64 MiB of HBM per device.

```python
import math
import jax
import jax.numpy as jnp
from jax import lax

S = 600
NT = 420
K = 64
COLS = 128
SWEEPS = 6
R = 32
ROWS = 8
P_SIZE = 1024
N_PAR = 8


def draw_freqs(key, part):
    shuffled = jax.random.permutation(key, NT // 2 - 3)[:K - 2] + 2
    ends = jnp.array([1, NT // 2 - 1], dtype=jnp.int32)
    return jnp.concatenate([ends, shuffled.astype(jnp.int32)])


def shard_levels(stream_key, extent, pieces, low, high):
    loudness = 1.0
    for dim, blocks in pieces:
        draws = jax.random.uniform(jax.random.fold_in(jax.random.fold_in(stream_key, 6), dim), (blocks,), jnp.float32, low / len(pieces), high / len(pieces))
        loudness = loudness * jnp.repeat(jnp.exp(draws), extent[dim] // blocks).reshape((-1,) + (1,) * (len(extent) - 1 - dim))
    return loudness


def noise(rng, extent, spread, bound, shards=(), kind=jnp.bfloat16):
    drawn = spread * jax.random.normal(rng, extent, jnp.float32)
    if shards:
        drawn = drawn * shard_levels(rng, extent, shards, -0.22, 0.18)
    return jnp.clip(drawn, -bound, bound).astype(kind)


def setup_inputs(seed: int = 0) -> dict:
    splits = jax.random.split(jax.random.key(seed), 7)
    data = noise(splits[0], (R, S, NT), 1.0, 6.0, ((1, 4),))
    green = noise(splits[1], (K, S, 2, P_SIZE), (2 * S) ** -0.5, 0.1875, ((1, 4), (3, 8)))
    freqs = draw_freqs(jax.random.fold_in(splits[6], 71), 0)
    sensor_order = jax.random.permutation(splits[3], S).astype(jnp.int32)
    kappa = jnp.clip(jnp.exp(math.log(0.5) - 2.3025851 * jax.random.uniform(splits[4], (ROWS, COLS), jnp.float32) ** shard_levels(splits[4], (ROWS, COLS), ((0, 8),), -0.2, 0.2)), 0.05, 0.5)
    theta = jnp.clip(jnp.exp(math.log(2.0) - 1.3862944 * jax.random.uniform(splits[5], (ROWS, COLS), jnp.float32) ** shard_levels(splits[5], (ROWS, COLS), ((0, 8),), -0.2, 0.2)), 0.5, 2.0)
    return dict(data=data, green=green, freqs=freqs, sensor_order=sensor_order, kappa=kappa, theta=theta)


lower_bound = 0.05
upper_bound = 16.5

def make_tables(freqs):
    times = jnp.arange(NT, dtype=jnp.int32)
    phase = times[:, None] * freqs[None, :] % NT
    angle = phase.astype(jnp.float32) * (2.0 * math.pi / NT)
    cosine = jnp.cos(angle)
    sine = jnp.sin(angle)
    forward = (jnp.concatenate([cosine, -sine], axis=1) / math.sqrt(NT)).astype(jnp.bfloat16)
    inverse = (jnp.concatenate([cosine, -sine], axis=1) / math.sqrt(K)).astype(jnp.bfloat16)
    return (forward, inverse)

def chebyshev_scalars():
    center = 0.5 * (upper_bound + lower_bound)
    radius = 0.5 * (upper_bound - lower_bound)
    alphas = []
    betas = []
    alpha = 1.0 / center
    for sweep_index in range(SWEEPS):
        if sweep_index == 0:
            alpha = 1.0 / center
            beta = 0.0
        else:
            if sweep_index == 1:
                beta = 0.5 * (radius * alpha) ** 2
            else:
                beta = (radius * alpha / 2.0) ** 2
            alpha = 1.0 / (center - beta / alpha)
        alphas.append(alpha)
        betas.append(beta)
    return (alphas, betas)

def face_terms(theta):
    padded = jnp.pad(theta, 1, mode='edge')
    north = 0.5 * (theta + padded[:-2, 1:-1])
    south = 0.5 * (theta + padded[2:, 1:-1])
    west = 0.5 * (theta + padded[1:-1, :-2])
    east = 0.5 * (theta + padded[1:-1, 2:])
    return (north, south, west, east)

def reference(data, green, freqs, sensor_order, kappa, theta):
    forward, inverse = make_tables(freqs)
    hp = lax.Precision.HIGHEST
    spectra = jnp.einsum('rst,tj->rsj', data.astype(jnp.float32), forward.astype(jnp.float32), precision=hp).astype(jnp.bfloat16)
    slotted = jnp.take(spectra, sensor_order, axis=1)

    def one_frequency(index):
        block = lax.dynamic_index_in_dim(green, index, 0, keepdims=False).astype(jnp.float32)
        real_data = lax.dynamic_index_in_dim(slotted, index, 2, keepdims=False).astype(jnp.float32)
        imag_data = lax.dynamic_index_in_dim(slotted, index + K, 2, keepdims=False).astype(jnp.float32)
        real_green = block[:, 0, :]
        imag_green = block[:, 1, :]
        real_part = jnp.dot(real_data, real_green, precision=hp) + jnp.dot(imag_data, imag_green, precision=hp)
        imag_part = jnp.dot(imag_data, real_green, precision=hp) - jnp.dot(real_data, imag_green, precision=hp)
        return (real_part, imag_part)
    real_all, imag_all = lax.map(one_frequency, jnp.arange(K, dtype=jnp.int32))
    adjoint = jnp.concatenate([jnp.transpose(real_all, (1, 0, 2)), jnp.transpose(imag_all, (1, 0, 2))], axis=1)
    adjoint_b = adjoint.astype(jnp.bfloat16)
    field = jnp.einsum('tj,rjp->rtp', inverse.astype(jnp.float32), adjoint_b.astype(jnp.float32), precision=hp)
    grid = field.reshape(R, NT, N_PAR, ROWS, COLS // N_PAR)
    grid = jnp.transpose(grid, (0, 1, 3, 4, 2)).reshape(R, NT, ROWS, COLS)
    north, south, west, east = face_terms(theta)
    diagonal = kappa + north + south + west + east

    def operator(field_in):
        padded = jnp.pad(field_in, ((0, 0), (0, 0), (1, 1), (1, 1)))
        return diagonal * field_in - north * padded[:, :, :-2, 1:-1] - south * padded[:, :, 2:, 1:-1] - west * padded[:, :, 1:-1, :-2] - east * padded[:, :, 1:-1, 2:]
    alphas, betas = chebyshev_scalars()
    solution = jnp.zeros_like(grid)
    residual = grid
    direction = grid
    for sweep_index in range(SWEEPS):
        if sweep_index == 0:
            direction = residual
        else:
            direction = residual + betas[sweep_index] * direction
        solution = solution + alphas[sweep_index] * direction
        if sweep_index + 1 < SWEEPS:
            residual = residual - alphas[sweep_index] * operator(direction)
    return solution.astype(jnp.bfloat16)
```

```python
import functools
import math

import jax
import jax.numpy as jnp
from jax import lax
from jax.experimental import pallas as pl
from jax.experimental.pallas import tpu as pltpu
from jax.sharding import PartitionSpec as P

NT = 420
SWEEPS = 6
lower_bound = 0.05
upper_bound = 16.5
MESH = pl.DeviceIdType.MESH
F32 = jnp.float32
BF16 = jnp.bfloat16


def chebyshev_scalars():
    center = 0.5 * (upper_bound + lower_bound)
    radius = 0.5 * (upper_bound - lower_bound)
    alphas = []
    betas = []
    alpha = 1.0 / center
    for sweep_index in range(SWEEPS):
        if sweep_index == 0:
            alpha = 1.0 / center
            beta = 0.0
        else:
            if sweep_index == 1:
                beta = 0.5 * (radius * alpha) ** 2
            else:
                beta = (radius * alpha / 2.0) ** 2
            alpha = 1.0 / (center - beta / alpha)
        alphas.append(alpha)
        betas.append(beta)
    return (alphas, betas)


def iota(shape, dim):
    return lax.broadcasted_iota(jnp.int32, shape, dim)


def round_up(value, unit):
    return -(-value // unit) * unit


def kernel(
    n_sens, n_par, probes, sensors, kper,
    data_hbm, green_hbm, wf, wi, order, kappa, theta,
    out,
    data_v, green_v, green_f, green_s, spec_f, ubuf, vbuf, vt, part, rsbuf, adj, gin,
    coef, ysend, sin, sf,
    load_sem, u_send, u_recv, z_send, z_recv, x_send, x_recv, rs_send, rs_recv,
    a_send, a_recv, c_send, c_recv, y_send, y_recv,
):
    a = lax.axis_index("sens")
    b = lax.axis_index("par")
    nz = n_par // 2
    zpos = b // 2
    xpos = b % 2
    here = probes // n_sens
    lanes = here * 2 * kper
    fields = kper * 2 * here
    spad = ubuf.shape[1]
    groups = n_sens
    width = out.shape[-1]
    cg = width // n_par

    def sens_peer(e):
        return {"sens": (a + e) % n_sens}

    def par_peer(e):
        return {"par": (b + e) % n_par}

    barrier = pltpu.get_barrier_semaphore()
    for e in range(1, n_sens):
        pl.semaphore_signal(barrier, inc=1, device_id=sens_peer(e), device_id_type=MESH)
    for e in range(1, n_par):
        pl.semaphore_signal(barrier, inc=1, device_id=par_peer(e), device_id_type=MESH)

    chunks = data_v.shape[0]
    loads = []
    for c in range(chunks):
        load = pltpu.make_async_copy(data_hbm.at[c], data_v.at[c], load_sem.at[c])
        load.start()
        loads.append(load)
    green_load = pltpu.make_async_copy(green_hbm, green_v, load_sem.at[chunks])
    green_load.start()

    pick = (iota((width, width), 0) // n_par + b * cg == iota((width, width), 1)).astype(F32)
    own = iota((n_par, width), 1) % n_par == iota((n_par, width), 0)
    for index, ref in enumerate((kappa, theta)):
        spread = jnp.where(own, jnp.broadcast_to(ref[...], (n_par, width)), 0.0)
        coef[0, index] = jnp.dot(spread, pick, precision=lax.Precision.HIGHEST, preferred_element_type=F32)

    rows = data_v.shape[1]
    wide = wf.shape[1]
    keep = iota((rows // here, here, wide), 2) // (2 * kper) == iota((rows // here, here, wide), 1)
    for c in range(chunks):
        loads[c].wait()
        prod = jnp.dot(data_v[c], wf[...], preferred_element_type=F32)
        prod = jnp.where(keep, prod.reshape(rows // here, here, wide), 0.0)
        spec_f[c * (rows // here):(c + 1) * (rows // here), :] = jnp.sum(prod, axis=1)
    ubuf[0, spad - 16:, :] = jnp.zeros((16, groups * lanes), BF16)
    for g in range(groups):
        ubuf[0, :sensors, g * lanes:(g + 1) * lanes] = spec_f[pl.ds(g, sensors, stride=groups), :][:, :lanes].astype(BF16)

    pl.semaphore_wait(barrier, n_sens + n_par - 2)
    sends = []

    def push(src, dst, ssem, rsem, peer):
        copy = pltpu.make_async_remote_copy(
            src_ref=src, dst_ref=dst, send_sem=ssem, recv_sem=rsem, device_id=peer, device_id_type=MESH
        )
        copy.start()
        sends.append(copy)
        return copy

    u_copies = [push(ubuf.at[0], ubuf.at[e], u_send.at[e], u_recv.at[e], sens_peer(e)) for e in range(1, n_sens)]
    c_copies = [push(coef.at[0], coef.at[e], c_send.at[e], c_recv.at[e], par_peer(e)) for e in range(1, n_par)]

    green_load.wait()
    green_s[:, spad - 16:, :] = jnp.zeros((green_s.shape[0], 16, green_s.shape[2]), BF16)

    def split(block, carry):
        green_f[...] = green_v[block].astype(F32)
        for k in range(kper):
            for c in range(2):
                piece = green_f[pl.ds(k * 2 * sensors + c, sensors, stride=2), :]
                green_s[block * kper + k, :sensors, c * width:(c + 1) * width] = piece.astype(BF16)
        return carry

    lax.fori_loop(0, n_par, split, 0)

    picked = jnp.zeros((spad, groups * lanes), F32)
    wanted = jnp.broadcast_to(order[...], (spad, spad))
    for e in range(n_sens):
        if e:
            u_copies[e - 1].wait_recv()
        base = ((a - e + n_sens) % n_sens) * sensors
        position = iota((spad, spad), 1)
        match = ((wanted == position + base) & (position < sensors)).astype(F32).astype(BF16)
        picked = picked + jnp.dot(match, ubuf[e], preferred_element_type=F32)
    vbuf[0, 0] = picked.astype(BF16)

    partner = {"par": zpos * 2 + (1 - xpos)}
    z_copies = {}
    x_copies = {}
    for d in range(1, nz):
        peer = {"par": ((zpos + d) % nz) * 2 + xpos}
        z_copies[d] = push(vbuf.at[0, 0], vbuf.at[d, 0], z_send.at[d], z_recv.at[d], peer)
    x_copies[0] = push(vbuf.at[0, 0], vbuf.at[0, 1], x_send.at[0], x_recv.at[0], partner)

    rs_copies = {}
    a_copies = []
    steps = [(d, xi) for d in range(nz) for xi in range(2)]

    def owner(step):
        d, xi = step
        other = xpos if xi == 0 else 1 - xpos
        return ((zpos - d + nz) % nz) * 2 + other

    def products(index):
        d, xi = steps[index]
        if xi:
            x_copies[d].wait_recv()
        elif d:
            z_copies[d].wait_recv()
            x_copies[d] = push(vbuf.at[d, 0], vbuf.at[d, 1], x_send.at[d], x_recv.at[d], partner)
        block = owner(steps[index])
        for t in range(vt.shape[0]):
            size = min(spad - t * 128, 128)
            vt[t, :, :size] = jnp.transpose(vbuf[d, xi, t * 128:t * 128 + size, :].astype(F32))
        half = probes
        for k in range(kper):
            left = []
            for t in range(vt.shape[0]):
                real = vt[t, pl.ds(k, half, stride=2 * kper), :]
                imag = vt[t, pl.ds(kper + k, half, stride=2 * kper), :]
                left.append(jnp.concatenate([real, imag], axis=0).astype(BF16)[:, :min(spad - t * 128, 128)])
            left = jnp.concatenate(left, axis=1)
            prod = jnp.dot(left, green_s[block * kper + k], preferred_element_type=F32)
            re = prod[:half, :width] + prod[half:, width:]
            im = prod[half:, :width] - prod[:half, width:]
            for g in range(groups):
                both = jnp.concatenate([re[g * here:(g + 1) * here], im[g * here:(g + 1) * here]], axis=0)
                part[index, g, k * 2 * here:(k + 1) * 2 * here, :] = both.astype(BF16)
        rs_copies[index] = [
            push(
                part.at[index, (a + e) % n_sens], rsbuf.at[index, e - 1],
                rs_send.at[index, e - 1], rs_recv.at[index, e - 1], sens_peer(e),
            )
            for e in range(1, n_sens)
        ]

    def reduce(index):
        for copy in rs_copies[index]:
            copy.wait_recv()
        total = part[index, a].astype(F32)
        for e in range(1, n_sens):
            total = total + rsbuf[index, e - 1].astype(F32)
        if index == 0:
            gin[b] = total.astype(BF16)
        else:
            adj[index] = total.astype(BF16)
            a_copies.append(
                push(adj.at[index], gin.at[b], a_send.at[index], a_recv.at[index], {"par": owner(steps[index])})
            )

    for index in range(n_par):
        products(index)
        if index:
            reduce(index - 1)
    reduce(n_par - 1)

    for copy in c_copies:
        copy.wait_recv()
    kap = coef[0, 0]
    tht = coef[0, 1]
    for e in range(1, n_par):
        kap = kap + coef[e, 0]
        tht = tht + coef[e, 1]
    lane = iota((n_par, width), 1)
    sub = iota((n_par, width), 0)
    first_row = lane < cg
    last_row = lane >= width - cg
    first_col = (sub == 0) & (lane % cg == 0)
    last_col = (sub == n_par - 1) & (lane % cg == cg - 1)
    up = pltpu.roll(tht, cg, 1)
    down = pltpu.roll(tht, width - cg, 1)
    left_of = jnp.concatenate([pltpu.roll(tht, 1, 1)[n_par - 1:], tht[:n_par - 1]], axis=0)
    right_of = jnp.concatenate([tht[1:], pltpu.roll(tht, width - 1, 1)[:1]], axis=0)
    north = 0.5 * (tht + jnp.where(first_row, tht, up))
    south = 0.5 * (tht + jnp.where(last_row, tht, down))
    west = 0.5 * (tht + jnp.where(first_col, tht, left_of))
    east = 0.5 * (tht + jnp.where(last_col, tht, right_of))
    diagonal = kap + north + south + west + east
    north = jnp.where(first_row, 0.0, north)
    south = jnp.where(last_row, 0.0, south)
    west = jnp.where(first_col, 0.0, west)
    east = jnp.where(last_col, 0.0, east)
    for index, value in enumerate((diagonal, north, south, west, east)):
        sf[index * n_par:(index + 1) * n_par, :] = value

    for copy in a_copies:
        copy.wait_recv()
    alphas, betas = chebyshev_scalars()
    tile = 16

    def row(index, block):
        return jnp.broadcast_to(sf[index * n_par + block:index * n_par + block + 1, :], (tile, width))

    def smooth(chunk, carry):
        start = pl.multiple_of(chunk * tile, tile)
        res = [gin[q, pl.ds(start, tile), :].astype(F32) for q in range(n_par)]
        dirn = res
        x = [alphas[0] * v for v in res]
        for sweep in range(1, SWEEPS):
            wrap_left = pltpu.roll(dirn[n_par - 1], 1, 1)
            wrap_right = pltpu.roll(dirn[0], width - 1, 1)
            fresh = []
            for q in range(n_par):
                u = dirn[q]
                w = dirn[q - 1] if q else wrap_left
                e = dirn[q + 1] if q + 1 < n_par else wrap_right
                value = (
                    row(0, q) * u
                    - row(1, q) * pltpu.roll(u, cg, 1)
                    - row(2, q) * pltpu.roll(u, width - cg, 1)
                    - row(3, q) * w
                    - row(4, q) * e
                )
                fresh.append(res[q] - alphas[sweep - 1] * value)
            res = fresh
            dirn = [r + betas[sweep] * v for r, v in zip(res, dirn)]
            x = [v + alphas[sweep] * u for v, u in zip(x, dirn)]
        place = iota((tile, width), 1) // cg
        for i in range(n_par):
            value = jnp.zeros((tile, width), F32)
            for q in range(n_par):
                shift = ((q - i) % n_par) * cg
                moved = pltpu.roll(x[q], shift, 1) if shift else x[q]
                value = jnp.where(place == q, moved, value)
            ysend[i, pl.ds(start, tile), :] = value.astype(BF16)
        return carry

    lax.fori_loop(0, fields // tile, smooth, 0)

    y_copies = []
    for e in range(1, n_par):
        target = (b + e) % n_par
        y_copies.append(push(ysend.at[target], sin.at[b], y_send.at[e], y_recv.at[e], {"par": target}))
    sin[b] = ysend[b]
    source = iota((width, width), 0)
    perm = ((source % cg) * n_par + source // cg == iota((width, width), 1)).astype(F32).astype(BF16)
    for copy in y_copies:
        copy.wait_recv()
    for q in range(n_par):
        sf[q * fields:(q + 1) * fields, :] = jnp.dot(sin[q], perm, preferred_element_type=F32)
    for r in range(here):
        freq_rows = sf[pl.ds(r, n_par * fields // here, stride=here), :].astype(BF16)
        out[r] = jnp.dot(wi[...], freq_rows, preferred_element_type=F32).astype(BF16)
    for copy in sends:
        copy.wait_send()


def table(freqs, negative_sine, scale):
    times = jnp.arange(NT, dtype=jnp.int32)
    phase = times[:, None] * freqs[None, :] % NT
    angle = phase.astype(F32) * (2.0 * math.pi / NT)
    return (jnp.where(negative_sine[None, :], -jnp.sin(angle), jnp.cos(angle)) / math.sqrt(scale)).astype(BF16)


def local(n_sens, n_par, data, green, freqs, sensor_order, kappa, theta):
    probes, sensors, _ = data.shape
    nfreq, _, _, cells = green.shape
    width = kappa.shape[1]
    kper = nfreq // n_par
    here = probes // n_sens
    lanes = here * 2 * kper
    fields = kper * 2 * here
    spad = round_up(sensors, 16)
    mine = lax.dynamic_slice_in_dim(freqs, lax.axis_index("par") * kper, kper)
    wide = round_up(lanes, 128)
    wf = table(jnp.tile(mine, wide // kper), jnp.arange(wide) // kper % 2 == 1, NT)
    wi = table(jnp.repeat(freqs, 2), jnp.arange(2 * nfreq) % 2 == 1, nfreq)
    chunks = 3
    flat = jnp.transpose(data, (1, 0, 2)).reshape(chunks, sensors * probes // chunks, NT)
    blocks = green.reshape(n_par, kper * sensors * 2, cells)
    order = jnp.pad(sensor_order, (0, spad - sensors), constant_values=-1).reshape(spad, 1)
    vmem = pl.BlockSpec(memory_space=pltpu.VMEM)
    anywhere = pl.BlockSpec(memory_space=pl.ANY)
    dma = pltpu.SemaphoreType.DMA
    nz = n_par // 2
    block = 2 * kper * here
    out = pl.pallas_call(
        functools.partial(kernel, n_sens, n_par, probes, sensors, kper),
        out_shape=jax.ShapeDtypeStruct((here, NT, width), BF16),
        in_specs=[anywhere, anywhere] + [vmem] * 5,
        out_specs=vmem,
        scratch_shapes=[
            pltpu.VMEM(flat.shape, BF16),
            pltpu.VMEM(blocks.shape, BF16),
            pltpu.VMEM(blocks.shape[1:], F32),
            pltpu.VMEM((nfreq, spad, 2 * cells), BF16),
            pltpu.VMEM((sensors * n_sens, wide), F32),
            pltpu.VMEM((n_sens, spad, n_sens * lanes), BF16),
            pltpu.VMEM((nz, 2, spad, n_sens * lanes), BF16),
            pltpu.VMEM((round_up(spad, 128) // 128, n_sens * lanes, 128), F32),
            pltpu.VMEM((n_par, n_sens, block, cells), BF16),
            pltpu.VMEM((n_par, n_sens - 1, block, cells), BF16),
            pltpu.VMEM((n_par, block, cells), BF16),
            pltpu.VMEM((n_par, block, cells), BF16),
            pltpu.VMEM((n_par, 2, n_par, width), F32),
            pltpu.VMEM((n_par, block, width), BF16),
            pltpu.VMEM((n_par, block, width), BF16),
            pltpu.VMEM((n_par * block, width), F32),
            dma((chunks + 1,)),
            dma((n_sens,)), dma((n_sens,)),
            dma((nz,)), dma((nz,)),
            dma((nz,)), dma((nz,)),
            dma((n_par, n_sens - 1)), dma((n_par, n_sens - 1)),
            dma((n_par,)), dma((n_par,)),
            dma((n_par,)), dma((n_par,)),
            dma((n_par,)), dma((n_par,)),
        ],
        compiler_params=pltpu.CompilerParams(
            collective_id=0, has_side_effects=True, vmem_limit_bytes=56 * 1024 * 1024
        ),
    )(flat, blocks, wf, wi, order, kappa, theta)
    return out.reshape(here, NT, 1, width)


def solution(mesh):
    placed = (
        P(None, "sens", None),
        P(None, "sens", None, "par"),
        P(),
        P("sens"),
        P("par", None),
        P("par", None),
    )
    return jax.shard_map(
        functools.partial(local, mesh.shape["sens"], mesh.shape["par"]),
        mesh=mesh, in_specs=placed, out_specs=P("sens", None, "par", None), check_vma=False,
    )
```

```python
import functools
import math

import jax
import jax.numpy as jnp
from jax import lax
from jax.experimental import pallas as pl
from jax.experimental.pallas import tpu as pltpu
from jax.sharding import PartitionSpec as P

SWEEPS = 6
lower_bound = 0.05
upper_bound = 16.5
MESH = pl.DeviceIdType.MESH
F32 = jnp.float32
BF16 = jnp.bfloat16


def chebyshev_scalars():
    center = 0.5 * (upper_bound + lower_bound)
    radius = 0.5 * (upper_bound - lower_bound)
    alphas = []
    betas = []
    alpha = 1.0 / center
    for sweep_index in range(SWEEPS):
        if sweep_index == 0:
            alpha = 1.0 / center
            beta = 0.0
        else:
            if sweep_index == 1:
                beta = 0.5 * (radius * alpha) ** 2
            else:
                beta = (radius * alpha / 2.0) ** 2
            alpha = 1.0 / (center - beta / alpha)
        alphas.append(alpha)
        betas.append(beta)
    return (alphas, betas)


def iota(shape, dim):
    return lax.broadcasted_iota(jnp.int32, shape, dim)


def round_up(value, unit):
    return -(-value // unit) * unit


def ring_place(z, size):
    odd = z % 2
    return odd * ((z + 1) // 2) + (1 - odd) * ((size - z // 2) % size)


def ring_member(place, size):
    back = ((place + size - 1) % size) // max(size // 2, 1)
    return (1 - back) * (2 * place - 1) + back * (2 * ((size - place) % size))


def table(freqs, chosen, quarter, nt, scale):
    lanes_freq = jnp.dot(freqs, chosen, preferred_element_type=F32)[:1]
    shape = (nt, chosen.shape[1])
    turn = iota(shape, 0).astype(F32) * lanes_freq + quarter.astype(F32) * (nt // 4)
    turn = turn - nt * jnp.floor((turn + 0.5) * (1.0 / nt))
    arc = (nt // 4 - jnp.abs(turn - nt // 2)) * (2.0 * math.pi / nt)
    square = arc * arc
    sine = jnp.full(shape, 1.0 / math.factorial(13), F32)
    for power in (11, 9, 7, 5, 3, 1):
        sign = -1.0 if power % 4 == 3 else 1.0
        sine = sine * square + sign / math.factorial(power)
    return (sine * arc * (-1.0 / math.sqrt(scale))).astype(BF16)


def kernel(
    n_sens, n_par, probes, sensors, kper,
    data_hbm, green_hbm, freqs, order, kappa, theta,
    out,
    wf, wi, tall, data_v, green_v, green_f, green_s, spec_f, ubuf, vbuf, vt, part, rsbuf, adj, gin,
    coef, ysend, sin, sf,
    load_sem, u_send, u_recv, z_send, z_recv, x_send, x_recv, rs_send, rs_recv,
    a_send, a_recv, c_send, c_recv, y_send, y_recv,
):
    a = lax.axis_index("sens")
    b = lax.axis_index("par")
    nz = n_par // 2
    xpos = b % 2
    zring = ring_place(b // 2, nz)
    here = probes // n_sens
    lanes = here * 2 * kper
    fields = kper * 2 * here
    spad = ubuf.shape[2]
    groups = n_sens
    width = out.shape[-1]
    cg = width // n_par

    def sens_peer(e):
        return {"sens": (a + e) % n_sens}

    def par_peer(e):
        return {"par": (b + e) % n_par}

    barrier = pltpu.get_barrier_semaphore()
    for e in range(1, n_sens):
        pl.semaphore_signal(barrier, inc=1, device_id=sens_peer(e), device_id_type=MESH)
    for e in range(1, n_par):
        pl.semaphore_signal(barrier, inc=1, device_id=par_peer(e), device_id_type=MESH)

    chunks = data_v.shape[0]
    loads = []
    for c in range(chunks):
        load = pltpu.make_async_copy(data_hbm.at[c], data_v.at[c], load_sem.at[c])
        load.start()
        loads.append(load)
    green_load = pltpu.make_async_copy(green_hbm, green_v, load_sem.at[chunks])
    green_load.start()

    nt = wi.shape[0]
    nfreq = freqs.shape[1]
    freq_rows = jnp.broadcast_to(freqs[...], (8, nfreq)).astype(F32).astype(BF16)
    wide = wf.shape[1]
    chosen = iota((nfreq, wide), 0) == b * kper + iota((nfreq, wide), 1) % kper
    wf[...] = table(freq_rows, chosen.astype(F32).astype(BF16), iota((nt, wide), 1) // kper % 2, nt, nt)

    pick = (iota((width, width), 0) // n_par + b * cg == iota((width, width), 1)).astype(F32)
    own = iota((n_par, width), 1) % n_par == iota((n_par, width), 0)
    for index, ref in enumerate((kappa, theta)):
        spread = jnp.where(own, jnp.broadcast_to(ref[...], (n_par, width)), 0.0)
        coef[0, index] = jnp.dot(spread, pick, precision=lax.Precision.HIGHEST, preferred_element_type=F32)

    rows = data_v.shape[1]
    keep = iota((rows // here, here, wide), 2) // (2 * kper) == iota((rows // here, here, wide), 1)
    for c in range(chunks):
        loads[c].wait()
        prod = jnp.dot(data_v[c], wf[...], preferred_element_type=F32)
        prod = jnp.where(keep, prod.reshape(rows // here, here, wide), 0.0)
        spec_f[c * (rows // here):(c + 1) * (rows // here), :] = jnp.sum(prod, axis=1)
    ubuf[0, 0, spad - 16:, :] = jnp.zeros((16, groups * lanes), BF16)
    for g in range(groups):
        ubuf[0, 0, :sensors, g * lanes:(g + 1) * lanes] = spec_f[pl.ds(g, sensors, stride=groups), :][:, :lanes].astype(BF16)

    pl.semaphore_wait(barrier, n_sens + n_par - 2)
    sends = []

    def push(src, dst, ssem, rsem, peer):
        copy = pltpu.make_async_remote_copy(
            src_ref=src, dst_ref=dst, send_sem=ssem, recv_sem=rsem, device_id=peer, device_id_type=MESH
        )
        copy.start()
        sends.append(copy)
        return copy

    ny = n_sens // 2
    cpos = a % 2
    yring = ring_place(a // 2, ny)
    core_peer = {"sens": (a // 2) * 2 + (1 - cpos)}
    y_next = {"sens": ring_member((yring + 1) % ny, ny) * 2 + cpos}
    u_copies = {}

    def gather_u(d):
        if d:
            u_copies[d, 0].wait_recv()
        if d + 1 < ny:
            u_copies[d + 1, 0] = push(ubuf.at[d, 0], ubuf.at[d + 1, 0], u_send.at[d, 0], u_recv.at[d + 1, 0], y_next)
        u_copies[d, 1] = push(ubuf.at[d, 0], ubuf.at[d, 1], u_send.at[d, 1], u_recv.at[d, 1], core_peer)

    gather_u(0)
    c_copies = [push(coef.at[0], coef.at[e], c_send.at[e], c_recv.at[e], par_peer(e)) for e in range(1, n_par)]

    green_load.wait()
    green_s[:, spad - 16:, :] = jnp.zeros((green_s.shape[0], 16, green_s.shape[2]), BF16)

    def split(block, carry):
        green_f[...] = green_v[block].astype(F32)
        for k in range(kper):
            for c in range(2):
                piece = green_f[pl.ds(k * 2 * sensors + c, sensors, stride=2), :]
                green_s[block * kper + k, :sensors, c * width:(c + 1) * width] = piece.astype(BF16)
        return carry

    lax.fori_loop(0, n_par, split, 0)

    column = jnp.transpose(jnp.broadcast_to(order[...].astype(F32), (128, sensors)))[:, :1]
    wanted = jnp.broadcast_to(column, (sensors, spad))
    picked = jnp.zeros((sensors, groups * lanes), F32)
    position = iota((sensors, spad), 1)
    for d in range(ny):
        if d:
            gather_u(d)
        for ci in range(2):
            if ci:
                u_copies[d, 1].wait_recv()
            source = ring_member((yring - d + ny) % ny, ny) * 2 + (cpos if ci == 0 else 1 - cpos)
            match = (wanted == (position + source * sensors).astype(F32)) & (position < sensors)
            picked = picked + jnp.dot(match.astype(F32).astype(BF16), ubuf[d, ci], preferred_element_type=F32)
    vbuf[0, 0, spad - 16:, :] = jnp.zeros((16, groups * lanes), BF16)
    vbuf[0, 0, :sensors, :] = picked.astype(BF16)

    partner = {"par": (b // 2) * 2 + (1 - xpos)}
    z_next = {"par": ring_member((zring + 1) % nz, nz) * 2 + xpos}
    cut = round_up(spad // 2, 16) if nz > 2 else spad
    z_copies = {}
    x_copies = {}

    def gather_v(d):
        if d:
            z_copies[d].wait_recv()
        if d + 1 < nz:
            z_copies[d + 1] = push(vbuf.at[d, 0], vbuf.at[d + 1, 0], z_send.at[d], z_recv.at[d + 1], z_next)
        size = cut if d + 1 == nz else spad
        x_copies[d] = push(
            vbuf.at[d, 0, pl.ds(0, size)], vbuf.at[d, 1, pl.ds(0, size)], x_send.at[d], x_recv.at[d], partner
        )

    gather_v(0)
    freq_pair = iota((nfreq, 2 * nfreq), 0) == iota((nfreq, 2 * nfreq), 1) // 2
    wi[...] = table(freq_rows, freq_pair.astype(F32).astype(BF16), iota((nt, 2 * nfreq), 1) % 2, nt, nfreq)

    rs_copies = {}
    a_copies = []
    steps = [(0, 0)]
    for d in range(1, nz):
        steps += [(d, 0), (d - 1, 1)]
    steps.append((nz - 1, 1))

    def owner(step):
        d, xi = step
        other = xpos if xi == 0 else 1 - xpos
        return ring_member((zring - d + nz) % nz, nz) * 2 + other

    def products(index):
        d, xi = steps[index]
        if xi:
            x_copies[d].wait_recv()
            if d + 2 == nz and cut < spad:
                rest = pl.ds(cut, spad - cut)
                z_copies[nz] = push(
                    vbuf.at[d, 1, rest], vbuf.at[d + 1, 1, rest], z_send.at[nz], z_recv.at[nz], z_next
                )
            if d + 1 == nz and cut < spad:
                z_copies[nz].wait_recv()
        elif d:
            gather_v(d)
        block = owner(steps[index])
        for t in range(vt.shape[0]):
            size = min(spad - t * 128, 128)
            vt[t, :, :size] = jnp.transpose(vbuf[d, xi, t * 128:t * 128 + size, :].astype(F32))
        half = probes
        for k in range(kper):
            left = []
            for t in range(vt.shape[0]):
                real = vt[t, pl.ds(k, half, stride=2 * kper), :]
                imag = vt[t, pl.ds(kper + k, half, stride=2 * kper), :]
                left.append(jnp.concatenate([real, imag], axis=0).astype(BF16)[:, :min(spad - t * 128, 128)])
            left = jnp.concatenate(left, axis=1)
            prod = jnp.dot(left, green_s[block * kper + k], preferred_element_type=F32)
            re = prod[:half, :width] + prod[half:, width:]
            im = prod[half:, :width] - prod[:half, width:]
            for g in range(groups):
                both = jnp.concatenate([re[g * here:(g + 1) * here], im[g * here:(g + 1) * here]], axis=0)
                part[index, g, k * 2 * here:(k + 1) * 2 * here, :] = both.astype(BF16)
        rs_copies[index] = [
            push(
                part.at[index, (a + e) % n_sens], rsbuf.at[index, e - 1],
                rs_send.at[index, e - 1], rs_recv.at[index, e - 1], sens_peer(e),
            )
            for e in range(1, n_sens)
        ]

    def reduce(index):
        for copy in rs_copies[index]:
            copy.wait_recv()
        total = part[index, a].astype(F32)
        for e in range(1, n_sens):
            total = total + rsbuf[index, e - 1].astype(F32)
        if index == 0:
            gin[b] = total.astype(BF16)
        else:
            adj[index] = total.astype(BF16)
            a_copies.append(
                push(adj.at[index], gin.at[b], a_send.at[index], a_recv.at[index], {"par": owner(steps[index])})
            )

    for index in range(n_par):
        products(index)
        if index >= 2:
            reduce(index - 2)
    reduce(n_par - 2)
    reduce(n_par - 1)

    for copy in c_copies:
        copy.wait_recv()
    kap = coef[0, 0]
    tht = coef[0, 1]
    for e in range(1, n_par):
        kap = kap + coef[e, 0]
        tht = tht + coef[e, 1]
    lane = iota((n_par, width), 1)
    sub = iota((n_par, width), 0)
    first_row = lane < cg
    last_row = lane >= width - cg
    first_col = (sub == 0) & (lane % cg == 0)
    last_col = (sub == n_par - 1) & (lane % cg == cg - 1)
    up = pltpu.roll(tht, cg, 1)
    down = pltpu.roll(tht, width - cg, 1)
    left_of = jnp.concatenate([pltpu.roll(tht, 1, 1)[n_par - 1:], tht[:n_par - 1]], axis=0)
    right_of = jnp.concatenate([tht[1:], pltpu.roll(tht, width - 1, 1)[:1]], axis=0)
    north = 0.5 * (tht + jnp.where(first_row, tht, up))
    south = 0.5 * (tht + jnp.where(last_row, tht, down))
    west = 0.5 * (tht + jnp.where(first_col, tht, left_of))
    east = 0.5 * (tht + jnp.where(last_col, tht, right_of))
    diagonal = kap + north + south + west + east
    north = jnp.where(first_row, 0.0, north)
    south = jnp.where(last_row, 0.0, south)
    west = jnp.where(first_col, 0.0, west)
    east = jnp.where(last_col, 0.0, east)
    for index, value in enumerate((diagonal, north, south, west, east)):
        sf[index * n_par:(index + 1) * n_par, :] = value

    for copy in a_copies:
        copy.wait_recv()
    alphas, betas = chebyshev_scalars()
    tile = 16
    low = 8

    def row(index, block):
        return jnp.broadcast_to(sf[index * n_par + block:index * n_par + block + 1, :], (low, width))

    def smooth(chunk, carry):
        start = pl.multiple_of(chunk * tile, tile)
        loaded = [gin[q, pl.ds(start, tile), :].astype(F32) for q in range(n_par)]
        place = iota((low, width), 1) // cg
        rows_out = []
        for part_index in range(tile // low):
            res = [v[part_index * low:(part_index + 1) * low] for v in loaded]
            dirn = res
            x = [alphas[0] * v for v in res]
            for sweep in range(1, SWEEPS):
                wrap_left = pltpu.roll(dirn[n_par - 1], 1, 1)
                wrap_right = pltpu.roll(dirn[0], width - 1, 1)
                fresh = []
                for q in range(n_par):
                    u = dirn[q]
                    w = dirn[q - 1] if q else wrap_left
                    e = dirn[q + 1] if q + 1 < n_par else wrap_right
                    value = (
                        row(0, q) * u
                        - row(1, q) * pltpu.roll(u, cg, 1)
                        - row(2, q) * pltpu.roll(u, width - cg, 1)
                        - row(3, q) * w
                        - row(4, q) * e
                    )
                    fresh.append(res[q] - alphas[sweep - 1] * value)
                res = fresh
                dirn = [r + betas[sweep] * v for r, v in zip(res, dirn)]
                x = [v + alphas[sweep] * u for v, u in zip(x, dirn)]
            moved_rows = []
            for i in range(n_par):
                value = x[i]
                for q in range(n_par):
                    if q != i:
                        value = jnp.where(place == q, pltpu.roll(x[q], ((q - i) % n_par) * cg, 1), value)
                moved_rows.append(value)
            rows_out.append(moved_rows)
        for i in range(n_par):
            both = jnp.concatenate([piece[i] for piece in rows_out], axis=0)
            ysend[i, pl.ds(start, tile), :] = both.astype(BF16)
        return carry

    cuts = [0, fields // tile // 2, fields // tile]
    y_copies = []
    for half in range(2):
        lax.fori_loop(cuts[half], cuts[half + 1], smooth, 0)
        span = pl.ds(cuts[half] * tile, (cuts[half + 1] - cuts[half]) * tile)
        for e in range(1, n_par):
            target = (b + e) % n_par
            y_copies.append(
                push(
                    ysend.at[target, span], sin.at[b, span],
                    y_send.at[half, e], y_recv.at[half, e], {"par": target},
                )
            )
    sin[b] = ysend[b]
    source = iota((width, width), 0)
    perm = ((source % cg) * n_par + source // cg == iota((width, width), 1)).astype(F32).astype(BF16)
    for copy in y_copies:
        copy.wait_recv()
    for q in range(n_par):
        sf[q * fields:(q + 1) * fields, :] = jnp.dot(sin[q], perm, preferred_element_type=F32)
    for r in range(here):
        mine = sf[pl.ds(r, n_par * fields // here, stride=here), :].astype(BF16)
        tall[pl.ds(r, nt, stride=here), :] = jnp.dot(wi[...], mine, preferred_element_type=F32)
    out[...] = tall[...].astype(BF16)
    for copy in sends:
        copy.wait_send()


def local(n_sens, n_par, data, green, freqs, sensor_order, kappa, theta):
    probes, sensors, nt = data.shape
    nfreq, _, _, cells = green.shape
    width = kappa.shape[1]
    kper = nfreq // n_par
    here = probes // n_sens
    lanes = here * 2 * kper
    fields = kper * 2 * here
    spad = round_up(sensors, 16)
    wide = round_up(lanes, 128)
    chunks = 3
    flat = jnp.transpose(data, (1, 0, 2)).reshape(chunks, sensors * probes // chunks, nt)
    blocks = green.reshape(n_par, kper * sensors * 2, cells)
    vmem = pl.BlockSpec(memory_space=pltpu.VMEM)
    anywhere = pl.BlockSpec(memory_space=pl.ANY)
    dma = pltpu.SemaphoreType.DMA
    nz = n_par // 2
    block = 2 * kper * here
    out = pl.pallas_call(
        functools.partial(kernel, n_sens, n_par, probes, sensors, kper),
        out_shape=jax.ShapeDtypeStruct((nt * here, width), BF16),
        in_specs=[anywhere, anywhere] + [vmem] * 4,
        out_specs=vmem,
        scratch_shapes=[
            pltpu.VMEM((nt, wide), BF16),
            pltpu.VMEM((nt, 2 * nfreq), BF16),
            pltpu.VMEM((nt * here, width), F32),
            pltpu.VMEM(flat.shape, BF16),
            pltpu.VMEM(blocks.shape, BF16),
            pltpu.VMEM(blocks.shape[1:], F32),
            pltpu.VMEM((nfreq, spad, 2 * cells), BF16),
            pltpu.VMEM((sensors * n_sens, wide), F32),
            pltpu.VMEM((n_sens // 2, 2, spad, n_sens * lanes), BF16),
            pltpu.VMEM((nz, 2, spad, n_sens * lanes), BF16),
            pltpu.VMEM((round_up(spad, 128) // 128, n_sens * lanes, 128), F32),
            pltpu.VMEM((n_par, n_sens, block, cells), BF16),
            pltpu.VMEM((n_par, n_sens - 1, block, cells), BF16),
            pltpu.VMEM((n_par, block, cells), BF16),
            pltpu.VMEM((n_par, block, cells), BF16),
            pltpu.VMEM((n_par, 2, n_par, width), F32),
            pltpu.VMEM((n_par, block, width), BF16),
            pltpu.VMEM((n_par, block, width), BF16),
            pltpu.VMEM((n_par * block, width), F32),
            dma((chunks + 1,)),
            dma((n_sens // 2, 2)), dma((n_sens // 2, 2)),
            dma((nz + 1,)), dma((nz + 1,)),
            dma((nz,)), dma((nz,)),
            dma((n_par, n_sens - 1)), dma((n_par, n_sens - 1)),
            dma((n_par,)), dma((n_par,)),
            dma((n_par,)), dma((n_par,)),
            dma((2, n_par)), dma((2, n_par)),
        ],
        compiler_params=pltpu.CompilerParams(
            collective_id=0, has_side_effects=True, vmem_limit_bytes=56 * 1024 * 1024
        ),
    )(flat, blocks, freqs.reshape(1, nfreq), sensor_order.reshape(1, sensors), kappa, theta)
    return jnp.transpose(out.reshape(nt, here, 1, width), (1, 0, 2, 3))


def solution(mesh):
    placed = (
        P(None, "sens", None),
        P(None, "sens", None, "par"),
        P(),
        P("sens"),
        P("par", None),
        P("par", None),
    )
    return jax.shard_map(
        functools.partial(local, mesh.shape["sens"], mesh.shape["par"]),
        mesh=mesh, in_specs=placed, out_specs=P("sens", None, "par", None), check_vma=False,
    )
```

```python
import functools
import math

import jax
import jax.numpy as jnp
from jax import lax
from jax.experimental import pallas as pl
from jax.experimental.pallas import tpu as pltpu
from jax.sharding import PartitionSpec as P

SWEEPS = 6
lower_bound = 0.05
upper_bound = 16.5
MESH = pl.DeviceIdType.MESH
F32 = jnp.float32
BF16 = jnp.bfloat16


def chebyshev_scalars():
    center = 0.5 * (upper_bound + lower_bound)
    radius = 0.5 * (upper_bound - lower_bound)
    alphas = []
    betas = []
    alpha = 1.0 / center
    for sweep_index in range(SWEEPS):
        if sweep_index == 0:
            alpha = 1.0 / center
            beta = 0.0
        else:
            if sweep_index == 1:
                beta = 0.5 * (radius * alpha) ** 2
            else:
                beta = (radius * alpha / 2.0) ** 2
            alpha = 1.0 / (center - beta / alpha)
        alphas.append(alpha)
        betas.append(beta)
    return (alphas, betas)


def iota(shape, dim):
    return lax.broadcasted_iota(jnp.int32, shape, dim)


def round_up(value, unit):
    return -(-value // unit) * unit


def ring_place(z, size):
    odd = z % 2
    return odd * ((z + 1) // 2) + (1 - odd) * ((size - z // 2) % size)


def ring_member(place, size):
    back = ((place + size - 1) % size) // max(size // 2, 1)
    return (1 - back) * (2 * place - 1) + back * (2 * ((size - place) % size))


def table(freqs, chosen, quarter, nt, scale):
    lanes_freq = jnp.dot(freqs, chosen, preferred_element_type=F32)[:1]
    shape = (nt, chosen.shape[1])
    turn = iota(shape, 0).astype(F32) * lanes_freq + quarter.astype(F32) * (nt // 4)
    turn = turn - nt * jnp.floor((turn + 0.5) * (1.0 / nt))
    arc = (nt // 4 - jnp.abs(turn - nt // 2)) * (2.0 * math.pi / nt)
    square = arc * arc
    sine = jnp.full(shape, 1.0 / math.factorial(13), F32)
    for power in (11, 9, 7, 5, 3, 1):
        sign = -1.0 if power % 4 == 3 else 1.0
        sine = sine * square + sign / math.factorial(power)
    return (sine * arc * (-1.0 / math.sqrt(scale))).astype(BF16)


def kernel(
    n_sens, n_par, probes, sensors, kper,
    data_hbm, green_hbm, freqs, order, kappa, theta,
    out, wi_out,
    wf, data_v, green_v, green_f, green_s, spec_f, ubuf, vbuf, vt, part, rsbuf, adj, gin,
    coef, ysend, sin, sf,
    load_sem, u_send, u_recv, z_send, z_recv, x_send, x_recv, rs_send, rs_recv,
    a_send, a_recv, c_send, c_recv, y_send, y_recv,
):
    a = lax.axis_index("sens")
    b = lax.axis_index("par")
    nz = n_par // 2
    xpos = b % 2
    zring = ring_place(b // 2, nz)
    here = probes // n_sens
    lanes = here * 2 * kper
    fields = kper * 2 * here
    spad = ubuf.shape[2]
    groups = n_sens
    width = out.shape[-1]
    cg = width // n_par

    def sens_peer(e):
        return {"sens": (a + e) % n_sens}

    def par_peer(e):
        return {"par": (b + e) % n_par}

    barrier = pltpu.get_barrier_semaphore()
    for e in range(1, n_sens):
        pl.semaphore_signal(barrier, inc=1, device_id=sens_peer(e), device_id_type=MESH)
    for e in range(1, n_par):
        pl.semaphore_signal(barrier, inc=1, device_id=par_peer(e), device_id_type=MESH)

    chunks = data_v.shape[0]
    loads = []
    for c in range(chunks):
        load = pltpu.make_async_copy(data_hbm.at[c], data_v.at[c], load_sem.at[c])
        load.start()
        loads.append(load)
    green_load = pltpu.make_async_copy(green_hbm, green_v, load_sem.at[chunks])
    green_load.start()

    nt = wf.shape[0]
    nfreq = freqs.shape[1]
    freq_rows = jnp.broadcast_to(freqs[...], (8, nfreq)).astype(F32).astype(BF16)
    wide = wf.shape[1]
    chosen = iota((nfreq, wide), 0) == b * kper + iota((nfreq, wide), 1) // (2 * here)
    wf[...] = table(freq_rows, chosen.astype(F32).astype(BF16), iota((nt, wide), 1) // here % 2, nt, nt)

    pick = (iota((width, width), 0) // n_par + b * cg == iota((width, width), 1)).astype(F32)
    own = iota((n_par, width), 1) % n_par == iota((n_par, width), 0)
    for index, ref in enumerate((kappa, theta)):
        spread = jnp.where(own, jnp.broadcast_to(ref[...], (n_par, width)), 0.0)
        coef[0, index] = jnp.dot(spread, pick, precision=lax.Precision.HIGHEST, preferred_element_type=F32)

    rows = data_v.shape[1]
    sensors_chunk = sensors // chunks
    stack = round_up(sensors_chunk, 8)
    qshape = (groups * stack, rows)
    add_rows = iota(qshape, 1) // here == iota(qshape, 0) % stack * groups + iota(qshape, 0) // stack
    add_rows = add_rows.astype(F32).astype(BF16)
    lane = iota((rows, wide), 1)
    keep = (lane % here == iota((rows, wide), 0) % here) & (lane < lanes)
    for c in range(chunks):
        loads[c].wait()
        prod = jnp.dot(data_v[c], wf[...], preferred_element_type=F32)
        prod = jnp.where(keep, prod, 0.0).astype(BF16)
        sums = jnp.dot(add_rows, prod, preferred_element_type=F32)
        for g in range(groups):
            spec_f[g, c * sensors_chunk:(c + 1) * sensors_chunk, :] = sums[g * stack:g * stack + sensors_chunk]
    ubuf[0, 0, spad - 16:, :] = jnp.zeros((16, groups * lanes), BF16)
    for g in range(groups):
        ubuf[0, 0, :sensors, g * lanes:(g + 1) * lanes] = spec_f[g][:, :lanes].astype(BF16)

    pl.semaphore_wait(barrier, n_sens + n_par - 2)
    sends = []

    def push(src, dst, ssem, rsem, peer):
        copy = pltpu.make_async_remote_copy(
            src_ref=src, dst_ref=dst, send_sem=ssem, recv_sem=rsem, device_id=peer, device_id_type=MESH
        )
        copy.start()
        sends.append(copy)
        return copy

    ny = n_sens // 2
    cpos = a % 2
    yring = ring_place(a // 2, ny)
    core_peer = {"sens": (a // 2) * 2 + (1 - cpos)}
    y_next = {"sens": ring_member((yring + 1) % ny, ny) * 2 + cpos}
    u_copies = {}

    def gather_u(d):
        if d:
            u_copies[d, 0].wait_recv()
        if d + 1 < ny:
            u_copies[d + 1, 0] = push(ubuf.at[d, 0], ubuf.at[d + 1, 0], u_send.at[d, 0], u_recv.at[d + 1, 0], y_next)
        u_copies[d, 1] = push(ubuf.at[d, 0], ubuf.at[d, 1], u_send.at[d, 1], u_recv.at[d, 1], core_peer)

    gather_u(0)
    c_copies = [push(coef.at[0], coef.at[e], c_send.at[e], c_recv.at[e], par_peer(e)) for e in range(1, n_par)]

    green_load.wait()
    green_s[:, spad - 16:, :] = jnp.zeros((green_s.shape[0], 16, green_s.shape[2]), BF16)

    def split(block, carry):
        green_f[...] = green_v[block].astype(F32)
        for k in range(kper):
            for c in range(2):
                piece = green_f[pl.ds(k * 2 * sensors + c, sensors, stride=2), :]
                green_s[block * kper + k, :sensors, c * width:(c + 1) * width] = piece.astype(BF16)
        return carry

    bounds = [n_par * d // ny for d in range(ny + 1)]
    for d in range(ny):
        if d:
            gather_u(d)
        lax.fori_loop(bounds[d], bounds[d + 1], split, 0)

    column = jnp.transpose(jnp.broadcast_to(order[...].astype(F32), (128, sensors)))[:, :1]
    wanted = jnp.broadcast_to(column, (sensors, spad))
    picked = jnp.zeros((sensors, groups * lanes), F32)
    position = iota((sensors, spad), 1)
    for d in range(ny):
        for ci in range(2):
            if ci:
                u_copies[d, 1].wait_recv()
            source = ring_member((yring - d + ny) % ny, ny) * 2 + (cpos if ci == 0 else 1 - cpos)
            match = (wanted == (position + source * sensors).astype(F32)) & (position < sensors)
            picked = picked + jnp.dot(match.astype(F32).astype(BF16), ubuf[d, ci], preferred_element_type=F32)
    vbuf[0, 0, spad - 16:, :] = jnp.zeros((16, groups * lanes), BF16)
    vbuf[0, 0, :sensors, :] = picked.astype(BF16)

    partner = {"par": (b // 2) * 2 + (1 - xpos)}
    z_next = {"par": ring_member((zring + 1) % nz, nz) * 2 + xpos}
    cut = round_up(spad // 2, 16) if nz > 2 else spad
    z_copies = {}
    x_copies = {}

    def gather_v(d):
        if d:
            z_copies[d].wait_recv()
        if d + 1 < nz:
            z_copies[d + 1] = push(vbuf.at[d, 0], vbuf.at[d + 1, 0], z_send.at[d], z_recv.at[d + 1], z_next)
        size = cut if d + 1 == nz else spad
        x_copies[d] = push(
            vbuf.at[d, 0, pl.ds(0, size)], vbuf.at[d, 1, pl.ds(0, size)], x_send.at[d], x_recv.at[d], partner
        )

    gather_v(0)
    freq_pair = iota((nfreq, 2 * nfreq), 0) == iota((nfreq, 2 * nfreq), 1) // 2
    wi = table(freq_rows, freq_pair.astype(F32).astype(BF16), iota((nt, 2 * nfreq), 1) % 2, nt, nfreq)
    steps_here = wi_out.shape[1]
    for p in range(wi_out.shape[0]):
        wi_out[p] = wi[p * steps_here:(p + 1) * steps_here]

    rs_copies = {}
    a_copies = []
    steps = [(0, 0)]
    for d in range(1, nz):
        steps += [(d, 0), (d - 1, 1)]
    steps.append((nz - 1, 1))

    def owner(step):
        d, xi = step
        other = xpos if xi == 0 else 1 - xpos
        return ring_member((zring - d + nz) % nz, nz) * 2 + other

    def products(index):
        d, xi = steps[index]
        if xi:
            x_copies[d].wait_recv()
            if d + 2 == nz and cut < spad:
                rest = pl.ds(cut, spad - cut)
                z_copies[nz] = push(
                    vbuf.at[d, 1, rest], vbuf.at[d + 1, 1, rest], z_send.at[nz], z_recv.at[nz], z_next
                )
            if d + 1 == nz and cut < spad:
                z_copies[nz].wait_recv()
        elif d:
            gather_v(d)
        block = owner(steps[index])
        vt[...] = jnp.transpose(vbuf[d, xi])
        pair = 2 * here
        for k in range(kper):
            left = jnp.concatenate(
                [vt[g * lanes + k * pair:g * lanes + (k + 1) * pair, :] for g in range(groups)], axis=0
            )
            prod = jnp.dot(left, green_s[block * kper + k], preferred_element_type=F32)
            for g in range(groups):
                real = prod[g * pair:g * pair + here]
                imag = prod[g * pair + here:(g + 1) * pair]
                re = real[:, :width] + imag[:, width:]
                im = imag[:, :width] - real[:, width:]
                part[index, g, k * pair:(k + 1) * pair, :] = jnp.concatenate([re, im], axis=0).astype(BF16)
        rs_copies[index] = [
            push(
                part.at[index, (a + e) % n_sens], rsbuf.at[index, e - 1],
                rs_send.at[index, e - 1], rs_recv.at[index, e - 1], sens_peer(e),
            )
            for e in range(1, n_sens)
        ]

    def reduce(index):
        for copy in rs_copies[index]:
            copy.wait_recv()
        total = part[index, a].astype(F32)
        for e in range(1, n_sens):
            total = total + rsbuf[index, e - 1].astype(F32)
        if index == 0:
            gin[b] = total.astype(BF16)
        else:
            adj[index] = total.astype(BF16)
            a_copies.append(
                push(adj.at[index], gin.at[b], a_send.at[index], a_recv.at[index], {"par": owner(steps[index])})
            )

    for index in range(n_par):
        products(index)
        if index >= 2:
            reduce(index - 2)
    reduce(n_par - 2)
    reduce(n_par - 1)

    for copy in c_copies:
        copy.wait_recv()
    kap = coef[0, 0]
    tht = coef[0, 1]
    for e in range(1, n_par):
        kap = kap + coef[e, 0]
        tht = tht + coef[e, 1]
    lane = iota((n_par, width), 1)
    sub = iota((n_par, width), 0)
    first_row = lane < cg
    last_row = lane >= width - cg
    first_col = (sub == 0) & (lane % cg == 0)
    last_col = (sub == n_par - 1) & (lane % cg == cg - 1)
    up = pltpu.roll(tht, cg, 1)
    down = pltpu.roll(tht, width - cg, 1)
    left_of = jnp.concatenate([pltpu.roll(tht, 1, 1)[n_par - 1:], tht[:n_par - 1]], axis=0)
    right_of = jnp.concatenate([tht[1:], pltpu.roll(tht, width - 1, 1)[:1]], axis=0)
    north = 0.5 * (tht + jnp.where(first_row, tht, up))
    south = 0.5 * (tht + jnp.where(last_row, tht, down))
    west = 0.5 * (tht + jnp.where(first_col, tht, left_of))
    east = 0.5 * (tht + jnp.where(last_col, tht, right_of))
    diagonal = kap + north + south + west + east
    north = jnp.where(first_row, 0.0, north)
    south = jnp.where(last_row, 0.0, south)
    west = jnp.where(first_col, 0.0, west)
    east = jnp.where(last_col, 0.0, east)
    for index, value in enumerate((diagonal, north, south, west, east)):
        sf[index * n_par:(index + 1) * n_par, :] = value

    for copy in a_copies:
        copy.wait_recv()
    alphas, betas = chebyshev_scalars()
    tile = 16
    low = 8

    def row(index, block):
        return jnp.broadcast_to(sf[index * n_par + block:index * n_par + block + 1, :], (low, width))

    def smooth(chunk, carry):
        start = pl.multiple_of(chunk * tile, tile)
        loaded = [gin[q, pl.ds(start, tile), :].astype(F32) for q in range(n_par)]
        place = iota((low, width), 1) // cg
        rows_out = []
        for part_index in range(tile // low):
            res = [v[part_index * low:(part_index + 1) * low] for v in loaded]
            dirn = res
            x = [alphas[0] * v for v in res]
            for sweep in range(1, SWEEPS):
                wrap_left = pltpu.roll(dirn[n_par - 1], 1, 1)
                wrap_right = pltpu.roll(dirn[0], width - 1, 1)
                fresh = []
                for q in range(n_par):
                    u = dirn[q]
                    w = dirn[q - 1] if q else wrap_left
                    e = dirn[q + 1] if q + 1 < n_par else wrap_right
                    value = (
                        row(0, q) * u
                        - row(1, q) * pltpu.roll(u, cg, 1)
                        - row(2, q) * pltpu.roll(u, width - cg, 1)
                        - row(3, q) * w
                        - row(4, q) * e
                    )
                    fresh.append(res[q] - alphas[sweep - 1] * value)
                res = fresh
                dirn = [r + betas[sweep] * v for r, v in zip(res, dirn)]
                x = [v + alphas[sweep] * u for v, u in zip(x, dirn)]
            moved_rows = []
            for i in range(n_par):
                value = x[i]
                for q in range(n_par):
                    if q != i:
                        value = jnp.where(place == q, pltpu.roll(x[q], ((q - i) % n_par) * cg, 1), value)
                moved_rows.append(value)
            rows_out.append(moved_rows)
        for i in range(n_par):
            both = jnp.concatenate([piece[i] for piece in rows_out], axis=0)
            ysend[i, pl.ds(start, tile), :] = both.astype(BF16)
        return carry

    cuts = [0, fields // tile // 2, fields // tile]
    y_copies = []
    for half in range(2):
        lax.fori_loop(cuts[half], cuts[half + 1], smooth, 0)
        span = pl.ds(cuts[half] * tile, (cuts[half + 1] - cuts[half]) * tile)
        for e in range(1, n_par):
            target = (b + e) % n_par
            y_copies.append(
                push(
                    ysend.at[target, span], sin.at[b, span],
                    y_send.at[half, e], y_recv.at[half, e], {"par": target},
                )
            )
    sin[b] = ysend[b]
    for copy in y_copies:
        copy.wait_recv()
    out[...] = sin[...]
    for copy in sends:
        copy.wait_send()


def inverse_kernel(n_par, here, smoothed, wi, out, sf, tall):
    width = out.shape[1]
    cg = width // n_par
    fields = smoothed.shape[0]

    @pl.when(pl.program_id(0) == 0)
    def _():
        source = iota((width, width), 0)
        perm = ((source % cg) * n_par + source // cg == iota((width, width), 1)).astype(F32).astype(BF16)
        sf[...] = jnp.dot(smoothed[...], perm, preferred_element_type=F32)

    steps = tall.shape[0] // here
    for r in range(here):
        mine = sf[pl.ds(r, fields // here, stride=here), :].astype(BF16)
        tall[pl.ds(r, steps, stride=here), :] = jnp.dot(wi[0], mine, preferred_element_type=F32)
    out[...] = tall[...].astype(BF16)


def local(n_sens, n_par, data, green, freqs, sensor_order, kappa, theta):
    probes, sensors, nt = data.shape
    nfreq, _, _, cells = green.shape
    width = kappa.shape[1]
    kper = nfreq // n_par
    here = probes // n_sens
    lanes = here * 2 * kper
    fields = kper * 2 * here
    spad = round_up(sensors, 16)
    wide = round_up(lanes, 128)
    chunks = 3
    pieces = 3
    flat = jnp.transpose(data, (1, 0, 2)).reshape(chunks, sensors * probes // chunks, nt)
    blocks = green.reshape(n_par, kper * sensors * 2, cells)
    vmem = pl.BlockSpec(memory_space=pltpu.VMEM)
    anywhere = pl.BlockSpec(memory_space=pl.ANY)
    dma = pltpu.SemaphoreType.DMA
    nz = n_par // 2
    block = 2 * kper * here
    smoothed, wi = pl.pallas_call(
        functools.partial(kernel, n_sens, n_par, probes, sensors, kper),
        out_shape=[
            jax.ShapeDtypeStruct((n_par, fields, width), BF16),
            jax.ShapeDtypeStruct((pieces, nt // pieces, 2 * nfreq), BF16),
        ],
        in_specs=[anywhere, anywhere] + [vmem] * 4,
        out_specs=[vmem, vmem],
        scratch_shapes=[
            pltpu.VMEM((nt, wide), BF16),
            pltpu.VMEM(flat.shape, BF16),
            pltpu.VMEM(blocks.shape, BF16),
            pltpu.VMEM(blocks.shape[1:], F32),
            pltpu.VMEM((nfreq, spad, 2 * cells), BF16),
            pltpu.VMEM((n_sens, sensors, wide), F32),
            pltpu.VMEM((n_sens // 2, 2, spad, n_sens * lanes), BF16),
            pltpu.VMEM((nz, 2, spad, n_sens * lanes), BF16),
            pltpu.VMEM((n_sens * lanes, spad), BF16),
            pltpu.VMEM((n_par, n_sens, block, cells), BF16),
            pltpu.VMEM((n_par, n_sens - 1, block, cells), BF16),
            pltpu.VMEM((n_par, block, cells), BF16),
            pltpu.VMEM((n_par, block, cells), BF16),
            pltpu.VMEM((n_par, 2, n_par, width), F32),
            pltpu.VMEM((n_par, block, width), BF16),
            pltpu.VMEM((n_par, block, width), BF16),
            pltpu.VMEM((n_par * block, width), F32),
            dma((chunks + 1,)),
            dma((n_sens // 2, 2)), dma((n_sens // 2, 2)),
            dma((nz + 1,)), dma((nz + 1,)),
            dma((nz,)), dma((nz,)),
            dma((n_par, n_sens - 1)), dma((n_par, n_sens - 1)),
            dma((n_par,)), dma((n_par,)),
            dma((n_par,)), dma((n_par,)),
            dma((2, n_par)), dma((2, n_par)),
        ],
        compiler_params=pltpu.CompilerParams(
            collective_id=0, has_side_effects=True, vmem_limit_bytes=56 * 1024 * 1024
        ),
    )(flat, blocks, freqs.reshape(1, nfreq), sensor_order.reshape(1, sensors), kappa, theta)
    total = n_par * fields
    out = pl.pallas_call(
        functools.partial(inverse_kernel, n_par, here),
        out_shape=jax.ShapeDtypeStruct((nt * here, width), BF16),
        grid=(pieces,),
        in_specs=[
            pl.BlockSpec((total, width), lambda i: (0, 0)),
            pl.BlockSpec((1, nt // pieces, 2 * nfreq), lambda i: (i, 0, 0)),
        ],
        out_specs=pl.BlockSpec((nt * here // pieces, width), lambda i: (i, 0)),
        scratch_shapes=[
            pltpu.VMEM((total, width), F32),
            pltpu.VMEM((nt * here // pieces, width), F32),
        ],
    )(smoothed.reshape(total, width), wi)
    return jnp.transpose(out.reshape(nt, here, 1, width), (1, 0, 2, 3))


def solution(mesh):
    placed = (
        P(None, "sens", None),
        P(None, "sens", None, "par"),
        P(),
        P("sens"),
        P("par", None),
        P("par", None),
    )
    return jax.shard_map(
        functools.partial(local, mesh.shape["sens"], mesh.shape["par"]),
        mesh=mesh, in_specs=placed, out_specs=P("sens", None, "par", None), check_vma=False,
    )
```

```python
import functools
import math

import jax
import jax.numpy as jnp
from jax import lax
from jax.experimental import pallas as pl
from jax.experimental.pallas import tpu as pltpu
from jax.sharding import PartitionSpec as P

SWEEPS = 6
lower_bound = 0.05
upper_bound = 16.5
MESH = pl.DeviceIdType.MESH
F32 = jnp.float32
BF16 = jnp.bfloat16


def chebyshev_scalars():
    center = 0.5 * (upper_bound + lower_bound)
    radius = 0.5 * (upper_bound - lower_bound)
    alphas = []
    betas = []
    alpha = 1.0 / center
    for sweep_index in range(SWEEPS):
        if sweep_index == 0:
            alpha = 1.0 / center
            beta = 0.0
        else:
            if sweep_index == 1:
                beta = 0.5 * (radius * alpha) ** 2
            else:
                beta = (radius * alpha / 2.0) ** 2
            alpha = 1.0 / (center - beta / alpha)
        alphas.append(alpha)
        betas.append(beta)
    return (alphas, betas)


def iota(shape, dim):
    return lax.broadcasted_iota(jnp.int32, shape, dim)


def round_up(value, unit):
    return -(-value // unit) * unit


def ring_place(z, size):
    odd = z % 2
    return odd * ((z + 1) // 2) + (1 - odd) * ((size - z // 2) % size)


def ring_member(place, size):
    back = ((place + size - 1) % size) // max(size // 2, 1)
    return (1 - back) * (2 * place - 1) + back * (2 * ((size - place) % size))


def table(freqs, chosen, quarter, nt, scale):
    lanes_freq = jnp.dot(freqs, chosen, preferred_element_type=F32)[:1]
    shape = (nt, chosen.shape[1])
    turn = iota(shape, 0).astype(F32) * lanes_freq + quarter.astype(F32) * (nt // 4)
    turn = turn - nt * jnp.floor((turn + 0.5) * (1.0 / nt))
    arc = (nt // 4 - jnp.abs(turn - nt // 2)) * (2.0 * math.pi / nt)
    square = arc * arc
    sine = jnp.full(shape, 1.0 / math.factorial(13), F32)
    for power in (11, 9, 7, 5, 3, 1):
        sign = -1.0 if power % 4 == 3 else 1.0
        sine = sine * square + sign / math.factorial(power)
    return (sine * arc * (-1.0 / math.sqrt(scale))).astype(BF16)


def kernel(
    n_sens, n_par, probes, sensors, kper,
    data_hbm, green_hbm, freqs, order, kappa, theta,
    out, wi_out,
    wf, data_v, green_v, green_f, green_s, spec_f, ubuf, vbuf, vt, part, rsbuf, adj, gin,
    coef, ysend, sin, sf,
    load_sem, u_send, u_recv, z_send, z_recv, x_send, x_recv, rs_send, rs_recv,
    a_send, a_recv, c_send, c_recv, y_send, y_recv,
):
    a = lax.axis_index("sens")
    b = lax.axis_index("par")
    nz = n_par // 2
    xpos = b % 2
    zring = ring_place(b // 2, nz)
    here = probes // n_sens
    lanes = here * 2 * kper
    fields = kper * 2 * here
    spad = ubuf.shape[2]
    groups = n_sens
    width = out.shape[-1]
    cg = width // n_par

    def sens_peer(e):
        return {"sens": (a + e) % n_sens}

    def par_peer(e):
        return {"par": (b + e) % n_par}

    barrier = pltpu.get_barrier_semaphore()
    for e in range(1, n_sens):
        pl.semaphore_signal(barrier, inc=1, device_id=sens_peer(e), device_id_type=MESH)
    for e in range(1, n_par):
        pl.semaphore_signal(barrier, inc=1, device_id=par_peer(e), device_id_type=MESH)

    chunks = data_v.shape[0]
    loads = []
    for c in range(chunks):
        load = pltpu.make_async_copy(data_hbm.at[c], data_v.at[c], load_sem.at[c])
        load.start()
        loads.append(load)
    green_load = pltpu.make_async_copy(green_hbm, green_v, load_sem.at[chunks])

    nt = wf.shape[0]
    nfreq = freqs.shape[1]
    freq_rows = jnp.broadcast_to(freqs[...], (8, nfreq)).astype(F32).astype(BF16)
    wide = wf.shape[1]
    chosen = iota((nfreq, wide), 0) == b * kper + iota((nfreq, wide), 1) // (2 * here)
    wf[...] = table(freq_rows, chosen.astype(F32).astype(BF16), iota((nt, wide), 1) // here % 2, nt, nt)

    pick = (iota((width, width), 0) // n_par + b * cg == iota((width, width), 1)).astype(F32)
    own = iota((n_par, width), 1) % n_par == iota((n_par, width), 0)
    for index, ref in enumerate((kappa, theta)):
        spread = jnp.where(own, jnp.broadcast_to(ref[...], (n_par, width)), 0.0)
        coef[0, index] = jnp.dot(spread, pick, precision=lax.Precision.HIGHEST, preferred_element_type=F32)

    rows = data_v.shape[1]
    sensors_chunk = sensors // chunks
    stack = round_up(sensors_chunk, 8)
    qshape = (groups * stack, rows)
    add_rows = iota(qshape, 1) // here == iota(qshape, 0) % stack * groups + iota(qshape, 0) // stack
    add_rows = add_rows.astype(F32).astype(BF16)
    lane = iota((rows, wide), 1)
    keep = (lane % here == iota((rows, wide), 0) % here) & (lane < lanes)
    marks = [(c * sensors_chunk) // 16 * 16 for c in range(chunks)] + [spad]
    spec_f[:, spad - 16:, :] = jnp.zeros((groups, 16, wide), F32)
    sends = []

    def push(src, dst, ssem, rsem, peer):
        copy = pltpu.make_async_remote_copy(
            src_ref=src, dst_ref=dst, send_sem=ssem, recv_sem=rsem, device_id=peer, device_id_type=MESH
        )
        copy.start()
        sends.append(copy)
        return copy

    ny = n_sens // 2
    cpos = a % 2
    yring = ring_place(a // 2, ny)
    core_peer = {"sens": (a // 2) * 2 + (1 - cpos)}
    y_next = {"sens": ring_member((yring + 1) % ny, ny) * 2 + cpos}
    u_copies = {}

    def gather_u(d, c):
        span = pl.ds(marks[c], marks[c + 1] - marks[c])
        if d:
            u_copies[d, 0, c].wait_recv()
        if d + 1 < ny:
            u_copies[d + 1, 0, c] = push(
                ubuf.at[d, 0, span], ubuf.at[d + 1, 0, span], u_send.at[d, 0, c], u_recv.at[d + 1, 0, c], y_next
            )
        u_copies[d, 1, c] = push(
            ubuf.at[d, 0, span], ubuf.at[d, 1, span], u_send.at[d, 1, c], u_recv.at[d, 1, c], core_peer
        )

    for c in range(chunks):
        loads[c].wait()
        if c + 1 == chunks:
            green_load.start()
        prod = jnp.dot(data_v[c], wf[...], preferred_element_type=F32)
        prod = jnp.where(keep, prod, 0.0).astype(BF16)
        sums = jnp.dot(add_rows, prod, preferred_element_type=F32)
        for g in range(groups):
            spec_f[g, c * sensors_chunk:(c + 1) * sensors_chunk, :] = sums[g * stack:g * stack + sensors_chunk]
        lo, hi = marks[c], marks[c + 1]
        for g in range(groups):
            ubuf[0, 0, lo:hi, g * lanes:(g + 1) * lanes] = spec_f[g, lo:hi, :][:, :lanes].astype(BF16)
        if c == 0:
            pl.semaphore_wait(barrier, n_sens + n_par - 2)
        gather_u(0, c)
    c_copies = [push(coef.at[0], coef.at[e], c_send.at[e], c_recv.at[e], par_peer(e)) for e in range(1, n_par)]

    green_s[:, spad - 16:, :] = jnp.zeros((green_s.shape[0], 16, green_s.shape[2]), BF16)

    def split(block):
        green_f[...] = green_v[block].astype(F32)
        for k in range(kper):
            for c in range(2):
                piece = green_f[pl.ds(k * 2 * sensors + c, sensors, stride=2), :]
                green_s[block * kper + k, :sensors, c * width:(c + 1) * width] = piece.astype(BF16)

    steps = [(0, 0)]
    for d in range(1, nz):
        steps += [(d, 0), (d - 1, 1)]
    steps.append((nz - 1, 1))

    def owner(step):
        d, xi = step
        other = xpos if xi == 0 else 1 - xpos
        return ring_member((zring - d + nz) % nz, nz) * 2 + other

    ready = 0
    green_load.wait()
    for d in range(1, ny):
        for c in range(chunks):
            gather_u(d, c)
            if c + 1 < chunks:
                split(owner(steps[ready]))
                ready += 1

    column = jnp.transpose(jnp.broadcast_to(order[...].astype(F32), (128, sensors)))[:, :1]
    wanted = jnp.broadcast_to(column, (sensors, spad))
    picked = jnp.zeros((sensors, groups * lanes), F32)
    position = iota((sensors, spad), 1)
    for d in range(ny):
        for ci in range(2):
            if ci:
                for c in range(chunks):
                    u_copies[d, 1, c].wait_recv()
            source = ring_member((yring - d + ny) % ny, ny) * 2 + (cpos if ci == 0 else 1 - cpos)
            match = (wanted == (position + source * sensors).astype(F32)) & (position < sensors)
            picked = picked + jnp.dot(match.astype(F32).astype(BF16), ubuf[d, ci], preferred_element_type=F32)
    vbuf[0, 0, spad - 16:, :] = jnp.zeros((16, groups * lanes), BF16)
    vbuf[0, 0, :sensors, :] = picked.astype(BF16)

    partner = {"par": (b // 2) * 2 + (1 - xpos)}
    z_next = {"par": ring_member((zring + 1) % nz, nz) * 2 + xpos}
    cut = round_up(spad // 2, 16) if nz > 2 else spad
    z_copies = {}
    x_copies = {}

    halves = [pl.ds(0, cut)] + ([pl.ds(cut, spad - cut)] if cut < spad else [])

    def gather_v(d):
        for p, span in enumerate(halves):
            if d:
                z_copies[d, p].wait_recv()
            if d + 1 < nz:
                z_copies[d + 1, p] = push(
                    vbuf.at[d, 0, span], vbuf.at[d + 1, 0, span], z_send.at[d, p], z_recv.at[d + 1, p], z_next
                )
            if d + 1 < nz or p == 0:
                x_copies[d, p] = push(
                    vbuf.at[d, 0, span], vbuf.at[d, 1, span], x_send.at[d, p], x_recv.at[d, p], partner
                )

    gather_v(0)
    freq_pair = iota((nfreq, 2 * nfreq), 0) == iota((nfreq, 2 * nfreq), 1) // 2
    wi = table(freq_rows, freq_pair.astype(F32).astype(BF16), iota((nt, 2 * nfreq), 1) % 2, nt, nfreq)
    steps_here = wi_out.shape[1]
    for p in range(wi_out.shape[0]):
        wi_out[p] = wi[p * steps_here:(p + 1) * steps_here]

    rs_copies = {}
    a_copies = []
    def products(index):
        d, xi = steps[index]
        if xi:
            for p, span in enumerate(halves):
                if (d, p) in x_copies:
                    x_copies[d, p].wait_recv()
                if d + 2 == nz and p == 1:
                    z_copies[nz, 1] = push(
                        vbuf.at[d, 1, span], vbuf.at[d + 1, 1, span], z_send.at[nz, 1], z_recv.at[nz, 1], z_next
                    )
                if d + 1 == nz and p == 1:
                    z_copies[nz, 1].wait_recv()
        elif d:
            gather_v(d)
        block = owner(steps[index])
        vt[...] = jnp.transpose(vbuf[d, xi])
        pair = 2 * here
        for k in range(kper):
            left = jnp.concatenate(
                [vt[g * lanes + k * pair:g * lanes + (k + 1) * pair, :] for g in range(groups)], axis=0
            )
            prod = jnp.dot(left, green_s[block * kper + k], preferred_element_type=F32)
            for g in range(groups):
                real = prod[g * pair:g * pair + here]
                imag = prod[g * pair + here:(g + 1) * pair]
                re = real[:, :width] + imag[:, width:]
                im = imag[:, :width] - real[:, width:]
                part[index, g, k * pair:(k + 1) * pair, :] = jnp.concatenate([re, im], axis=0).astype(BF16)
        rs_copies[index] = [
            push(
                part.at[index, (a + e) % n_sens], rsbuf.at[index, e - 1],
                rs_send.at[index, e - 1], rs_recv.at[index, e - 1], sens_peer(e),
            )
            for e in range(1, n_sens)
        ]

    def reduce(index):
        for copy in rs_copies[index]:
            copy.wait_recv()
        total = part[index, a].astype(F32)
        for e in range(1, n_sens):
            total = total + rsbuf[index, e - 1].astype(F32)
        if index == 0:
            gin[b] = total.astype(BF16)
        else:
            adj[index] = total.astype(BF16)
            a_copies.append(
                push(adj.at[index], gin.at[b], a_send.at[index], a_recv.at[index], {"par": owner(steps[index])})
            )

    for index in range(n_par):
        if index >= ready:
            split(owner(steps[index]))
        products(index)
        if index >= 2:
            reduce(index - 2)
    reduce(n_par - 2)
    reduce(n_par - 1)

    for copy in c_copies:
        copy.wait_recv()
    kap = coef[0, 0]
    tht = coef[0, 1]
    for e in range(1, n_par):
        kap = kap + coef[e, 0]
        tht = tht + coef[e, 1]
    lane = iota((n_par, width), 1)
    sub = iota((n_par, width), 0)
    first_row = lane < cg
    last_row = lane >= width - cg
    first_col = (sub == 0) & (lane % cg == 0)
    last_col = (sub == n_par - 1) & (lane % cg == cg - 1)
    up = pltpu.roll(tht, cg, 1)
    down = pltpu.roll(tht, width - cg, 1)
    left_of = jnp.concatenate([pltpu.roll(tht, 1, 1)[n_par - 1:], tht[:n_par - 1]], axis=0)
    right_of = jnp.concatenate([tht[1:], pltpu.roll(tht, width - 1, 1)[:1]], axis=0)
    north = 0.5 * (tht + jnp.where(first_row, tht, up))
    south = 0.5 * (tht + jnp.where(last_row, tht, down))
    west = 0.5 * (tht + jnp.where(first_col, tht, left_of))
    east = 0.5 * (tht + jnp.where(last_col, tht, right_of))
    diagonal = kap + north + south + west + east
    north = jnp.where(first_row, 0.0, north)
    south = jnp.where(last_row, 0.0, south)
    west = jnp.where(first_col, 0.0, west)
    east = jnp.where(last_col, 0.0, east)
    for index, value in enumerate((diagonal, north, south, west, east)):
        sf[index * n_par:(index + 1) * n_par, :] = value

    for copy in a_copies:
        copy.wait_recv()
    alphas, betas = chebyshev_scalars()
    tile = 16
    low = 8

    def row(index, block):
        return jnp.broadcast_to(sf[index * n_par + block:index * n_par + block + 1, :], (low, width))

    def smooth(chunk, carry):
        start = pl.multiple_of(chunk * tile, tile)
        loaded = [gin[q, pl.ds(start, tile), :].astype(F32) for q in range(n_par)]
        place = iota((low, width), 1) // cg
        rows_out = []
        for part_index in range(tile // low):
            res = [v[part_index * low:(part_index + 1) * low] for v in loaded]
            dirn = res
            x = [alphas[0] * v for v in res]
            for sweep in range(1, SWEEPS):
                wrap_left = pltpu.roll(dirn[n_par - 1], 1, 1)
                wrap_right = pltpu.roll(dirn[0], width - 1, 1)
                fresh = []
                for q in range(n_par):
                    u = dirn[q]
                    w = dirn[q - 1] if q else wrap_left
                    e = dirn[q + 1] if q + 1 < n_par else wrap_right
                    value = (
                        row(0, q) * u
                        - row(1, q) * pltpu.roll(u, cg, 1)
                        - row(2, q) * pltpu.roll(u, width - cg, 1)
                        - row(3, q) * w
                        - row(4, q) * e
                    )
                    fresh.append(res[q] - alphas[sweep - 1] * value)
                res = fresh
                dirn = [r + betas[sweep] * v for r, v in zip(res, dirn)]
                x = [v + alphas[sweep] * u for v, u in zip(x, dirn)]
            moved_rows = []
            for i in range(n_par):
                value = x[i]
                for q in range(n_par):
                    if q != i:
                        value = jnp.where(place == q, pltpu.roll(x[q], ((q - i) % n_par) * cg, 1), value)
                moved_rows.append(value)
            rows_out.append(moved_rows)
        for i in range(n_par):
            both = jnp.concatenate([piece[i] for piece in rows_out], axis=0)
            ysend[i, pl.ds(start, tile), :] = both.astype(BF16)
        return carry

    cuts = [0, fields // tile // 2, fields // tile]
    y_copies = []
    for half in range(2):
        lax.fori_loop(cuts[half], cuts[half + 1], smooth, 0)
        span = pl.ds(cuts[half] * tile, (cuts[half + 1] - cuts[half]) * tile)
        for e in range(1, n_par):
            target = (b + e) % n_par
            y_copies.append(
                push(
                    ysend.at[target, span], sin.at[b, span],
                    y_send.at[half, e], y_recv.at[half, e], {"par": target},
                )
            )
    sin[b] = ysend[b]
    for copy in y_copies:
        copy.wait_recv()
    out[...] = sin[...]
    for copy in sends:
        copy.wait_send()


def inverse_kernel(n_par, here, smoothed, wi, out, sf, tall):
    width = out.shape[1]
    cg = width // n_par
    fields = smoothed.shape[0]

    @pl.when(pl.program_id(0) == 0)
    def _():
        source = iota((width, width), 0)
        perm = ((source % cg) * n_par + source // cg == iota((width, width), 1)).astype(F32).astype(BF16)
        sf[...] = jnp.dot(smoothed[...], perm, preferred_element_type=F32)

    steps = tall.shape[0] // here
    for r in range(here):
        mine = sf[pl.ds(r, fields // here, stride=here), :].astype(BF16)
        tall[pl.ds(r, steps, stride=here), :] = jnp.dot(wi[0], mine, preferred_element_type=F32)
    out[...] = tall[...].astype(BF16)


def local(n_sens, n_par, data, green, freqs, sensor_order, kappa, theta):
    probes, sensors, nt = data.shape
    nfreq, _, _, cells = green.shape
    width = kappa.shape[1]
    kper = nfreq // n_par
    here = probes // n_sens
    lanes = here * 2 * kper
    fields = kper * 2 * here
    spad = round_up(sensors, 16)
    wide = round_up(lanes, 128)
    chunks = 3
    pieces = 3
    flat = jnp.transpose(data, (1, 0, 2)).reshape(chunks, sensors * probes // chunks, nt)
    blocks = green.reshape(n_par, kper * sensors * 2, cells)
    vmem = pl.BlockSpec(memory_space=pltpu.VMEM)
    anywhere = pl.BlockSpec(memory_space=pl.ANY)
    dma = pltpu.SemaphoreType.DMA
    nz = n_par // 2
    block = 2 * kper * here
    smoothed, wi = pl.pallas_call(
        functools.partial(kernel, n_sens, n_par, probes, sensors, kper),
        out_shape=[
            jax.ShapeDtypeStruct((n_par, fields, width), BF16),
            jax.ShapeDtypeStruct((pieces, nt // pieces, 2 * nfreq), BF16),
        ],
        in_specs=[anywhere, anywhere] + [vmem] * 4,
        out_specs=[vmem, vmem],
        scratch_shapes=[
            pltpu.VMEM((nt, wide), BF16),
            pltpu.VMEM(flat.shape, BF16),
            pltpu.VMEM(blocks.shape, BF16),
            pltpu.VMEM(blocks.shape[1:], F32),
            pltpu.VMEM((nfreq, spad, 2 * cells), BF16),
            pltpu.VMEM((n_sens, spad, wide), F32),
            pltpu.VMEM((n_sens // 2, 2, spad, n_sens * lanes), BF16),
            pltpu.VMEM((nz, 2, spad, n_sens * lanes), BF16),
            pltpu.VMEM((n_sens * lanes, spad), BF16),
            pltpu.VMEM((n_par, n_sens, block, cells), BF16),
            pltpu.VMEM((n_par, n_sens - 1, block, cells), BF16),
            pltpu.VMEM((n_par, block, cells), BF16),
            pltpu.VMEM((n_par, block, cells), BF16),
            pltpu.VMEM((n_par, 2, n_par, width), F32),
            pltpu.VMEM((n_par, block, width), BF16),
            pltpu.VMEM((n_par, block, width), BF16),
            pltpu.VMEM((n_par * block, width), F32),
            dma((chunks + 1,)),
            dma((n_sens // 2, 2, chunks)), dma((n_sens // 2, 2, chunks)),
            dma((nz + 1, 2)), dma((nz + 1, 2)),
            dma((nz, 2)), dma((nz, 2)),
            dma((n_par, n_sens - 1)), dma((n_par, n_sens - 1)),
            dma((n_par,)), dma((n_par,)),
            dma((n_par,)), dma((n_par,)),
            dma((2, n_par)), dma((2, n_par)),
        ],
        compiler_params=pltpu.CompilerParams(
            collective_id=0, has_side_effects=True, vmem_limit_bytes=56 * 1024 * 1024
        ),
    )(flat, blocks, freqs.reshape(1, nfreq), sensor_order.reshape(1, sensors), kappa, theta)
    total = n_par * fields
    out = pl.pallas_call(
        functools.partial(inverse_kernel, n_par, here),
        out_shape=jax.ShapeDtypeStruct((nt * here, width), BF16),
        grid=(pieces,),
        in_specs=[
            pl.BlockSpec((total, width), lambda i: (0, 0)),
            pl.BlockSpec((1, nt // pieces, 2 * nfreq), lambda i: (i, 0, 0)),
        ],
        out_specs=pl.BlockSpec((nt * here // pieces, width), lambda i: (i, 0)),
        scratch_shapes=[
            pltpu.VMEM((total, width), F32),
            pltpu.VMEM((nt * here // pieces, width), F32),
        ],
    )(smoothed.reshape(total, width), wi)
    return jnp.transpose(out.reshape(nt, here, 1, width), (1, 0, 2, 3))


def solution(mesh):
    placed = (
        P(None, "sens", None),
        P(None, "sens", None, "par"),
        P(),
        P("sens"),
        P("par", None),
        P("par", None),
    )
    return jax.shard_map(
        functools.partial(local, mesh.shape["sens"], mesh.shape["par"]),
        mesh=mesh, in_specs=placed, out_specs=P("sens", None, "par", None), check_vma=False,
    )
```

```python
import functools
import math

import jax
import jax.numpy as jnp
from jax import lax
from jax.experimental import pallas as pl
from jax.experimental.pallas import tpu as pltpu
from jax.sharding import PartitionSpec as P

SWEEPS = 6
lower_bound = 0.05
upper_bound = 16.5
MESH = pl.DeviceIdType.MESH
F32 = jnp.float32
BF16 = jnp.bfloat16


def chebyshev_scalars():
    center = 0.5 * (upper_bound + lower_bound)
    radius = 0.5 * (upper_bound - lower_bound)
    alphas = []
    betas = []
    alpha = 1.0 / center
    for sweep_index in range(SWEEPS):
        if sweep_index == 0:
            alpha = 1.0 / center
            beta = 0.0
        else:
            if sweep_index == 1:
                beta = 0.5 * (radius * alpha) ** 2
            else:
                beta = (radius * alpha / 2.0) ** 2
            alpha = 1.0 / (center - beta / alpha)
        alphas.append(alpha)
        betas.append(beta)
    return (alphas, betas)


def iota(shape, dim):
    return lax.broadcasted_iota(jnp.int32, shape, dim)


def round_up(value, unit):
    return -(-value // unit) * unit


def ring_place(z, size):
    odd = z % 2
    return odd * ((z + 1) // 2) + (1 - odd) * ((size - z // 2) % size)


def ring_member(place, size):
    back = ((place + size - 1) % size) // max(size // 2, 1)
    return (1 - back) * (2 * place - 1) + back * (2 * ((size - place) % size))


def table(freqs, chosen, quarter, nt, scale):
    lanes_freq = jnp.dot(freqs, chosen, preferred_element_type=F32)[:1]
    shape = (nt, chosen.shape[1])
    turn = iota(shape, 0).astype(F32) * lanes_freq + quarter.astype(F32) * (nt // 4)
    turn = turn - nt * jnp.floor((turn + 0.5) * (1.0 / nt))
    arc = (nt // 4 - jnp.abs(turn - nt // 2)) * (2.0 * math.pi / nt)
    square = arc * arc
    sine = jnp.full(shape, 1.0 / math.factorial(13), F32)
    for power in (11, 9, 7, 5, 3, 1):
        sign = -1.0 if power % 4 == 3 else 1.0
        sine = sine * square + sign / math.factorial(power)
    return (sine * arc * (-1.0 / math.sqrt(scale))).astype(BF16)


def kernel(
    n_sens, n_par, probes, sensors, kper,
    data_hbm, green_hbm, freqs, order, kappa, theta,
    out, wi_out,
    wf, data_v, green_v, green_f, green_s, spec_f, ubuf, vbuf, vt, part, rsbuf, adj, gin,
    coef, ysend, sin, sf,
    load_sem, u_send, u_recv, z_send, z_recv, x_send, x_recv, rs_send, rs_recv,
    a_send, a_recv, c_send, c_recv, y_send, y_recv,
):
    a = lax.axis_index("sens")
    b = lax.axis_index("par")
    nz = n_par // 2
    xpos = b % 2
    zring = ring_place(b // 2, nz)
    here = probes // n_sens
    lanes = here * 2 * kper
    fields = kper * 2 * here
    spad = ubuf.shape[2]
    groups = n_sens
    width = out.shape[-1]
    cg = width // n_par

    def sens_peer(e):
        return {"sens": (a + e) % n_sens}

    def par_peer(e):
        return {"par": (b + e) % n_par}

    barrier = pltpu.get_barrier_semaphore()
    for e in range(1, n_sens):
        pl.semaphore_signal(barrier, inc=1, device_id=sens_peer(e), device_id_type=MESH)
    for e in range(1, n_par):
        pl.semaphore_signal(barrier, inc=1, device_id=par_peer(e), device_id_type=MESH)

    chunks = data_v.shape[0]
    loads = []
    for c in range(chunks):
        load = pltpu.make_async_copy(data_hbm.at[c], data_v.at[c], load_sem.at[c])
        load.start()
        loads.append(load)
    green_load = pltpu.make_async_copy(green_hbm, green_v, load_sem.at[chunks])

    nt = wf.shape[0]
    nfreq = freqs.shape[1]
    freq_rows = jnp.broadcast_to(freqs[...], (8, nfreq)).astype(F32).astype(BF16)
    wide = wf.shape[1]
    chosen = iota((nfreq, wide), 0) == b * kper + iota((nfreq, wide), 1) // (2 * here)
    wf[...] = table(freq_rows, chosen.astype(F32).astype(BF16), iota((1, wide), 1) // here % 2, nt, nt)

    pick = (iota((width, width), 0) // n_par + b * cg == iota((width, width), 1)).astype(F32)
    own = iota((n_par, width), 1) % n_par == iota((n_par, width), 0)
    for index, ref in enumerate((kappa, theta)):
        spread = jnp.where(own, jnp.broadcast_to(ref[...], (n_par, width)), 0.0)
        coef[0, index] = jnp.dot(spread, pick, precision=lax.Precision.HIGHEST, preferred_element_type=F32)

    rows = data_v.shape[1]
    sensors_chunk = sensors // chunks
    stack = round_up(sensors_chunk, 8)
    pile = groups * stack
    place = iota((pile, 1), 0)
    place = place % stack * groups + place // stack
    group_of = iota((1, rows), 1) // here
    add_rows = jnp.broadcast_to(place, (pile, rows)) == jnp.broadcast_to(group_of, (pile, rows))
    add_rows = add_rows.astype(F32).astype(BF16)
    lane = iota((1, here, wide), 2)
    keep = (lane % here == iota((1, here, wide), 1)) & (lane < lanes)
    marks = [(c * sensors_chunk) // 16 * 16 for c in range(chunks)] + [spad]
    spec_f[:, spad - 16:, :] = jnp.zeros((groups, 16, wide), F32)
    sends = []

    def push(src, dst, ssem, rsem, peer):
        copy = pltpu.make_async_remote_copy(
            src_ref=src, dst_ref=dst, send_sem=ssem, recv_sem=rsem, device_id=peer, device_id_type=MESH
        )
        copy.start()
        sends.append(copy)
        return copy

    ny = n_sens // 2
    cpos = a % 2
    yring = ring_place(a // 2, ny)
    core_peer = {"sens": (a // 2) * 2 + (1 - cpos)}
    y_next = {"sens": ring_member((yring + 1) % ny, ny) * 2 + cpos}
    u_copies = {}

    def gather_u(d, c):
        span = pl.ds(marks[c], marks[c + 1] - marks[c])
        if d:
            u_copies[d, 0, c].wait_recv()
        if d + 1 < ny:
            u_copies[d + 1, 0, c] = push(
                ubuf.at[d, 0, span], ubuf.at[d + 1, 0, span], u_send.at[d, 0, c], u_recv.at[d + 1, 0, c], y_next
            )
        u_copies[d, 1, c] = push(
            ubuf.at[d, 0, span], ubuf.at[d, 1, span], u_send.at[d, 1, c], u_recv.at[d, 1, c], core_peer
        )

    for c in range(chunks):
        loads[c].wait()
        if c + 1 == chunks:
            green_load.start()
        prod = jnp.dot(data_v[c], wf[...], preferred_element_type=F32)
        prod = jnp.where(keep, prod.reshape(rows // here, here, wide), 0.0).reshape(rows, wide).astype(BF16)
        sums = jnp.dot(add_rows, prod, preferred_element_type=F32)
        for g in range(groups):
            spec_f[g, c * sensors_chunk:(c + 1) * sensors_chunk, :] = sums[g * stack:g * stack + sensors_chunk]
        lo, hi = marks[c], marks[c + 1]
        for g in range(groups):
            ubuf[0, 0, lo:hi, g * lanes:(g + 1) * lanes] = spec_f[g, lo:hi, :][:, :lanes].astype(BF16)
        if c == 0:
            pl.semaphore_wait(barrier, n_sens + n_par - 2)
        gather_u(0, c)
    c_copies = [push(coef.at[0], coef.at[e], c_send.at[e], c_recv.at[e], par_peer(e)) for e in range(1, n_par)]

    green_s[:, spad - 16:, :] = jnp.zeros((green_s.shape[0], 16, green_s.shape[2]), BF16)

    def split(block):
        green_f[...] = green_v[block].astype(F32)
        for k in range(kper):
            for c in range(2):
                piece = green_f[pl.ds(k * 2 * sensors + c, sensors, stride=2), :]
                green_s[block * kper + k, :sensors, c * width:(c + 1) * width] = piece.astype(BF16)

    steps = [(0, 0)]
    for d in range(1, nz):
        steps += [(d, 0), (d - 1, 1)]
    steps.append((nz - 1, 1))

    def owner(step):
        d, xi = step
        other = xpos if xi == 0 else 1 - xpos
        return ring_member((zring - d + nz) % nz, nz) * 2 + other

    ready = 0
    green_load.wait()
    for d in range(1, ny):
        for c in range(chunks):
            gather_u(d, c)
            if c + 1 < chunks:
                split(owner(steps[ready]))
                ready += 1

    column = jnp.transpose(jnp.broadcast_to(order[...].astype(F32), (128, sensors)))[:, :1]
    wanted = jnp.broadcast_to(column, (sensors, spad))
    picked = jnp.zeros((sensors, groups * lanes), F32)
    position = iota((sensors, spad), 1)
    for d in range(ny):
        for ci in range(2):
            if ci:
                for c in range(chunks):
                    u_copies[d, 1, c].wait_recv()
            source = ring_member((yring - d + ny) % ny, ny) * 2 + (cpos if ci == 0 else 1 - cpos)
            match = (wanted == (position + source * sensors).astype(F32)) & (position < sensors)
            picked = picked + jnp.dot(match.astype(F32).astype(BF16), ubuf[d, ci], preferred_element_type=F32)
    vbuf[0, 0, spad - 16:, :] = jnp.zeros((16, groups * lanes), BF16)
    vbuf[0, 0, :sensors, :] = picked.astype(BF16)

    partner = {"par": (b // 2) * 2 + (1 - xpos)}
    z_next = {"par": ring_member((zring + 1) % nz, nz) * 2 + xpos}
    cut = round_up(spad // 2, 16) if nz > 2 else spad
    z_copies = {}
    x_copies = {}

    halves = [pl.ds(0, cut)] + ([pl.ds(cut, spad - cut)] if cut < spad else [])

    def gather_v(d):
        for p, span in enumerate(halves):
            if d:
                z_copies[d, p].wait_recv()
            if d + 1 < nz:
                z_copies[d + 1, p] = push(
                    vbuf.at[d, 0, span], vbuf.at[d + 1, 0, span], z_send.at[d, p], z_recv.at[d + 1, p], z_next
                )
            if d + 1 < nz or p == 0:
                x_copies[d, p] = push(
                    vbuf.at[d, 0, span], vbuf.at[d, 1, span], x_send.at[d, p], x_recv.at[d, p], partner
                )

    gather_v(0)
    freq_pair = iota((nfreq, 2 * nfreq), 0) == iota((nfreq, 2 * nfreq), 1) // 2
    wi = table(freq_rows, freq_pair.astype(F32).astype(BF16), iota((1, 2 * nfreq), 1) % 2, nt, nfreq)
    steps_here = wi_out.shape[1]
    for p in range(wi_out.shape[0]):
        wi_out[p] = wi[p * steps_here:(p + 1) * steps_here]

    rs_copies = {}
    a_copies = []

    def products(index):
        d, xi = steps[index]
        if xi:
            for p, span in enumerate(halves):
                if (d, p) in x_copies:
                    x_copies[d, p].wait_recv()
                if d + 2 == nz and p == 1:
                    z_copies[nz, 1] = push(
                        vbuf.at[d, 1, span], vbuf.at[d + 1, 1, span], z_send.at[nz, 1], z_recv.at[nz, 1], z_next
                    )
                if d + 1 == nz and p == 1:
                    z_copies[nz, 1].wait_recv()
        elif d:
            gather_v(d)
        block = owner(steps[index])
        vt[...] = jnp.transpose(vbuf[d, xi])
        pair = 2 * here
        for k in range(kper):
            left = jnp.concatenate(
                [vt[g * lanes + k * pair:g * lanes + (k + 1) * pair, :] for g in range(groups)], axis=0
            )
            prod = jnp.dot(left, green_s[block * kper + k], preferred_element_type=F32)
            for g in range(groups):
                real = prod[g * pair:g * pair + here]
                imag = prod[g * pair + here:(g + 1) * pair]
                re = real[:, :width] + imag[:, width:]
                im = imag[:, :width] - real[:, width:]
                part[index, g, k * pair:(k + 1) * pair, :] = jnp.concatenate([re, im], axis=0).astype(BF16)
        rs_copies[index] = [
            push(
                part.at[index, (a + e) % n_sens], rsbuf.at[index, e - 1],
                rs_send.at[index, e - 1], rs_recv.at[index, e - 1], sens_peer(e),
            )
            for e in range(1, n_sens)
        ]

    def reduce(index):
        for copy in rs_copies[index]:
            copy.wait_recv()
        total = part[index, a].astype(F32)
        for e in range(1, n_sens):
            total = total + rsbuf[index, e - 1].astype(F32)
        if index == 0:
            gin[b] = total.astype(BF16)
        else:
            adj[index] = total.astype(BF16)
            a_copies.append(
                push(adj.at[index], gin.at[b], a_send.at[index], a_recv.at[index], {"par": owner(steps[index])})
            )

    for index in range(n_par):
        if index >= ready:
            split(owner(steps[index]))
        products(index)
        if index >= 2:
            reduce(index - 2)
    reduce(n_par - 2)
    reduce(n_par - 1)

    for copy in c_copies:
        copy.wait_recv()
    kap = coef[0, 0]
    tht = coef[0, 1]
    for e in range(1, n_par):
        kap = kap + coef[e, 0]
        tht = tht + coef[e, 1]
    lane = iota((n_par, width), 1)
    sub = iota((n_par, width), 0)
    first_row = lane < cg
    last_row = lane >= width - cg
    first_col = (sub == 0) & (lane % cg == 0)
    last_col = (sub == n_par - 1) & (lane % cg == cg - 1)
    up = pltpu.roll(tht, cg, 1)
    down = pltpu.roll(tht, width - cg, 1)
    left_of = jnp.concatenate([pltpu.roll(tht, 1, 1)[n_par - 1:], tht[:n_par - 1]], axis=0)
    right_of = jnp.concatenate([tht[1:], pltpu.roll(tht, width - 1, 1)[:1]], axis=0)
    north = 0.5 * (tht + jnp.where(first_row, tht, up))
    south = 0.5 * (tht + jnp.where(last_row, tht, down))
    west = 0.5 * (tht + jnp.where(first_col, tht, left_of))
    east = 0.5 * (tht + jnp.where(last_col, tht, right_of))
    diagonal = kap + north + south + west + east
    north = jnp.where(first_row, 0.0, north)
    south = jnp.where(last_row, 0.0, south)
    west = jnp.where(first_col, 0.0, west)
    east = jnp.where(last_col, 0.0, east)
    for index, value in enumerate((diagonal, north, south, west, east)):
        sf[index * n_par:(index + 1) * n_par, :] = value

    for copy in a_copies:
        copy.wait_recv()
    alphas, betas = chebyshev_scalars()
    tile = 16
    low = 8

    def row(index, block):
        return jnp.broadcast_to(sf[index * n_par + block:index * n_par + block + 1, :], (low, width))

    def smooth(chunk, carry):
        start = pl.multiple_of(chunk * tile, tile)
        loaded = [gin[q, pl.ds(start, tile), :].astype(F32) for q in range(n_par)]
        place = iota((low, width), 1) // cg
        rows_out = []
        for part_index in range(tile // low):
            res = [v[part_index * low:(part_index + 1) * low] for v in loaded]
            dirn = res
            x = [alphas[0] * v for v in res]
            for sweep in range(1, SWEEPS):
                wrap_left = pltpu.roll(dirn[n_par - 1], 1, 1)
                wrap_right = pltpu.roll(dirn[0], width - 1, 1)
                fresh = []
                for q in range(n_par):
                    u = dirn[q]
                    w = dirn[q - 1] if q else wrap_left
                    e = dirn[q + 1] if q + 1 < n_par else wrap_right
                    value = (
                        row(0, q) * u
                        - row(1, q) * pltpu.roll(u, cg, 1)
                        - row(2, q) * pltpu.roll(u, width - cg, 1)
                        - row(3, q) * w
                        - row(4, q) * e
                    )
                    fresh.append(res[q] - alphas[sweep - 1] * value)
                res = fresh
                dirn = [r + betas[sweep] * v for r, v in zip(res, dirn)]
                x = [v + alphas[sweep] * u for v, u in zip(x, dirn)]
            moved_rows = []
            for i in range(n_par):
                value = x[i]
                for q in range(n_par):
                    if q != i:
                        value = jnp.where(place == q, pltpu.roll(x[q], ((q - i) % n_par) * cg, 1), value)
                moved_rows.append(value)
            rows_out.append(moved_rows)
        for i in range(n_par):
            both = jnp.concatenate([piece[i] for piece in rows_out], axis=0)
            ysend[i, pl.ds(start, tile), :] = both.astype(BF16)
        return carry

    cuts = [0, fields // tile // 2, fields // tile]
    y_copies = []
    for half in range(2):
        lax.fori_loop(cuts[half], cuts[half + 1], smooth, 0)
        span = pl.ds(cuts[half] * tile, (cuts[half + 1] - cuts[half]) * tile)
        for e in range(1, n_par):
            target = (b + e) % n_par
            y_copies.append(
                push(
                    ysend.at[target, span], sin.at[b, span],
                    y_send.at[half, e], y_recv.at[half, e], {"par": target},
                )
            )
    sin[b] = ysend[b]
    for copy in y_copies:
        copy.wait_recv()
    out[...] = sin[...]
    for copy in sends:
        copy.wait_send()


def inverse_kernel(n_par, here, smoothed, wi, out, sf, ordered, tall):
    width = out.shape[1]
    cg = width // n_par
    fields = smoothed.shape[0]

    @pl.when(pl.program_id(0) == 0)
    def _():
        source = iota((width, 1), 0)
        target = source % cg * n_par + source // cg
        perm = jnp.broadcast_to(target, (width, width)) == iota((width, width), 1)
        sf[...] = jnp.dot(smoothed[...], perm.astype(F32).astype(BF16), preferred_element_type=F32)
        for r in range(here):
            ordered[r] = sf[pl.ds(r, fields // here, stride=here), :].astype(BF16)

    steps = tall.shape[0] // here
    for r in range(here):
        tall[pl.ds(r, steps, stride=here), :] = jnp.dot(wi[0], ordered[r], preferred_element_type=F32)
    out[...] = tall[...].astype(BF16)


def local(n_sens, n_par, data, green, freqs, sensor_order, kappa, theta):
    probes, sensors, nt = data.shape
    nfreq, _, _, cells = green.shape
    width = kappa.shape[1]
    kper = nfreq // n_par
    here = probes // n_sens
    lanes = here * 2 * kper
    fields = kper * 2 * here
    spad = round_up(sensors, 16)
    wide = round_up(lanes, 128)
    chunks = 3
    pieces = 3
    flat = jnp.transpose(data, (1, 0, 2)).reshape(chunks, sensors * probes // chunks, nt)
    blocks = green.reshape(n_par, kper * sensors * 2, cells)
    vmem = pl.BlockSpec(memory_space=pltpu.VMEM)
    anywhere = pl.BlockSpec(memory_space=pl.ANY)
    dma = pltpu.SemaphoreType.DMA
    nz = n_par // 2
    block = 2 * kper * here
    smoothed, wi = pl.pallas_call(
        functools.partial(kernel, n_sens, n_par, probes, sensors, kper),
        out_shape=[
            jax.ShapeDtypeStruct((n_par, fields, width), BF16),
            jax.ShapeDtypeStruct((pieces, nt // pieces, 2 * nfreq), BF16),
        ],
        in_specs=[anywhere, anywhere] + [vmem] * 4,
        out_specs=[vmem, vmem],
        scratch_shapes=[
            pltpu.VMEM((nt, wide), BF16),
            pltpu.VMEM(flat.shape, BF16),
            pltpu.VMEM(blocks.shape, BF16),
            pltpu.VMEM(blocks.shape[1:], F32),
            pltpu.VMEM((nfreq, spad, 2 * cells), BF16),
            pltpu.VMEM((n_sens, spad, wide), F32),
            pltpu.VMEM((n_sens // 2, 2, spad, n_sens * lanes), BF16),
            pltpu.VMEM((nz, 2, spad, n_sens * lanes), BF16),
            pltpu.VMEM((n_sens * lanes, spad), BF16),
            pltpu.VMEM((n_par, n_sens, block, cells), BF16),
            pltpu.VMEM((n_par, n_sens - 1, block, cells), BF16),
            pltpu.VMEM((n_par, block, cells), BF16),
            pltpu.VMEM((n_par, block, cells), BF16),
            pltpu.VMEM((n_par, 2, n_par, width), F32),
            pltpu.VMEM((n_par, block, width), BF16),
            pltpu.VMEM((n_par, block, width), BF16),
            pltpu.VMEM((n_par * block, width), F32),
            dma((chunks + 1,)),
            dma((n_sens // 2, 2, chunks)), dma((n_sens // 2, 2, chunks)),
            dma((nz + 1, 2)), dma((nz + 1, 2)),
            dma((nz, 2)), dma((nz, 2)),
            dma((n_par, n_sens - 1)), dma((n_par, n_sens - 1)),
            dma((n_par,)), dma((n_par,)),
            dma((n_par,)), dma((n_par,)),
            dma((2, n_par)), dma((2, n_par)),
        ],
        compiler_params=pltpu.CompilerParams(
            collective_id=0, has_side_effects=True, vmem_limit_bytes=56 * 1024 * 1024
        ),
    )(flat, blocks, freqs.reshape(1, nfreq), sensor_order.reshape(1, sensors), kappa, theta)
    total = n_par * fields
    out = pl.pallas_call(
        functools.partial(inverse_kernel, n_par, here),
        out_shape=jax.ShapeDtypeStruct((nt * here, width), BF16),
        grid=(pieces,),
        in_specs=[
            pl.BlockSpec((total, width), lambda i: (0, 0)),
            pl.BlockSpec((1, nt // pieces, 2 * nfreq), lambda i: (i, 0, 0)),
        ],
        out_specs=pl.BlockSpec((nt * here // pieces, width), lambda i: (i, 0)),
        scratch_shapes=[
            pltpu.VMEM((total, width), F32),
            pltpu.VMEM((here, total // here, width), BF16),
            pltpu.VMEM((nt * here // pieces, width), F32),
        ],
    )(smoothed.reshape(total, width), wi)
    return jnp.transpose(out.reshape(nt, here, 1, width), (1, 0, 2, 3))


def solution(mesh):
    placed = (
        P(None, "sens", None),
        P(None, "sens", None, "par"),
        P(),
        P("sens"),
        P("par", None),
        P("par", None),
    )
    return jax.shard_map(
        functools.partial(local, mesh.shape["sens"], mesh.shape["par"]),
        mesh=mesh, in_specs=placed, out_specs=P("sens", None, "par", None), check_vma=False,
    )
```

```python
import functools
import math

import jax
import jax.numpy as jnp
from jax import lax
from jax.experimental import pallas as pl
from jax.experimental.pallas import tpu as pltpu
from jax.sharding import PartitionSpec as P

SWEEPS = 6
lower_bound = 0.05
upper_bound = 16.5
MESH = pl.DeviceIdType.MESH
F32 = jnp.float32
BF16 = jnp.bfloat16


def chebyshev_scalars():
    center = 0.5 * (upper_bound + lower_bound)
    radius = 0.5 * (upper_bound - lower_bound)
    alphas = []
    betas = []
    alpha = 1.0 / center
    for sweep_index in range(SWEEPS):
        if sweep_index == 0:
            alpha = 1.0 / center
            beta = 0.0
        else:
            if sweep_index == 1:
                beta = 0.5 * (radius * alpha) ** 2
            else:
                beta = (radius * alpha / 2.0) ** 2
            alpha = 1.0 / (center - beta / alpha)
        alphas.append(alpha)
        betas.append(beta)
    return (alphas, betas)


def iota(shape, dim):
    return lax.broadcasted_iota(jnp.int32, shape, dim)


def round_up(value, unit):
    return -(-value // unit) * unit


def ring_place(z, size):
    odd = z % 2
    return odd * ((z + 1) // 2) + (1 - odd) * ((size - z // 2) % size)


def ring_member(place, size):
    back = ((place + size - 1) % size) // max(size // 2, 1)
    return (1 - back) * (2 * place - 1) + back * (2 * ((size - place) % size))


def table(freqs, chosen, quarter, nt, scale):
    lanes_freq = jnp.dot(freqs, chosen, preferred_element_type=F32)[:1]
    shape = (nt, chosen.shape[1])
    turn = iota(shape, 0).astype(F32) * lanes_freq + quarter.astype(F32) * (nt // 4)
    turn = turn - nt * jnp.floor((turn + 0.5) * (1.0 / nt))
    arc = (nt // 4 - jnp.abs(turn - nt // 2)) * (2.0 * math.pi / nt)
    square = arc * arc
    sine = jnp.full(shape, 1.0 / math.factorial(13), F32)
    for power in (11, 9, 7, 5, 3, 1):
        sign = -1.0 if power % 4 == 3 else 1.0
        sine = sine * square + sign / math.factorial(power)
    return (sine * arc * (-1.0 / math.sqrt(scale))).astype(BF16)


def kernel(
    n_sens, n_par, probes, sensors, kper,
    data_hbm, green_hbm, freqs, order, kappa, theta,
    out, wi_out,
    wf, data_v, green_v, green_f, green_s, spec_f, ubuf, vbuf, vt, part, rsbuf, adj, gin,
    coef, ysend, sin, sf,
    load_sem, u_send, u_recv, z_send, z_recv, x_send, x_recv, rs_send, rs_recv,
    a_send, a_recv, c_send, c_recv, y_send, y_recv,
):
    a = lax.axis_index("sens")
    b = lax.axis_index("par")
    nz = n_par // 2
    xpos = b % 2
    zring = ring_place(b // 2, nz)
    here = probes // n_sens
    lanes = here * 2 * kper
    fields = kper * 2 * here
    spad = ubuf.shape[2]
    groups = n_sens
    width = out.shape[-1]
    cg = width // n_par

    def sens_peer(e):
        return {"sens": (a + e) % n_sens}

    def par_peer(e):
        return {"par": (b + e) % n_par}

    barrier = pltpu.get_barrier_semaphore()
    for e in range(1, n_sens):
        pl.semaphore_signal(barrier, inc=1, device_id=sens_peer(e), device_id_type=MESH)
    for e in range(1, n_par):
        pl.semaphore_signal(barrier, inc=1, device_id=par_peer(e), device_id_type=MESH)

    chunks = data_v.shape[0]
    loads = []
    for c in range(chunks):
        load = pltpu.make_async_copy(data_hbm.at[c], data_v.at[c], load_sem.at[c])
        load.start()
        loads.append(load)
    green_load = pltpu.make_async_copy(green_hbm, green_v, load_sem.at[chunks])

    nt = wf.shape[0]
    nfreq = freqs.shape[1]
    freq_rows = jnp.broadcast_to(freqs[...], (8, nfreq)).astype(F32).astype(BF16)
    wide = wf.shape[1]
    chosen = iota((nfreq, wide), 0) == b * kper + iota((nfreq, wide), 1) // (2 * here)
    wf[...] = table(freq_rows, chosen.astype(F32).astype(BF16), iota((1, wide), 1) // here % 2, nt, nt)

    pick = (iota((width, width), 0) // n_par + b * cg == iota((width, width), 1)).astype(F32)
    own = iota((n_par, width), 1) % n_par == iota((n_par, width), 0)
    for index, ref in enumerate((kappa, theta)):
        spread = jnp.where(own, jnp.broadcast_to(ref[...], (n_par, width)), 0.0)
        coef[0, index] = jnp.dot(spread, pick, precision=lax.Precision.HIGHEST, preferred_element_type=F32)

    rows = data_v.shape[1]
    sensors_chunk = sensors // chunks
    stack = round_up(sensors_chunk, 8)
    pile = groups * stack
    place = iota((pile, 1), 0)
    place = place % stack * groups + place // stack
    group_of = iota((1, rows), 1) // here
    add_rows = jnp.broadcast_to(place, (pile, rows)) == jnp.broadcast_to(group_of, (pile, rows))
    add_rows = add_rows.astype(F32).astype(BF16)
    lane = iota((1, here, wide), 2)
    keep = (lane % here == iota((1, here, wide), 1)) & (lane < lanes)
    marks = [(c * sensors_chunk) // 16 * 16 for c in range(chunks)] + [spad]
    spec_f[:, spad - 16:, :] = jnp.zeros((groups, 16, wide), F32)
    sends = []

    def push(src, dst, ssem, rsem, peer):
        copy = pltpu.make_async_remote_copy(
            src_ref=src, dst_ref=dst, send_sem=ssem, recv_sem=rsem, device_id=peer, device_id_type=MESH
        )
        copy.start()
        sends.append(copy)
        return copy

    ny = n_sens // 2
    cpos = a % 2
    yring = ring_place(a // 2, ny)
    core_peer = {"sens": (a // 2) * 2 + (1 - cpos)}
    y_next = {"sens": ring_member((yring + 1) % ny, ny) * 2 + cpos}
    u_copies = {}

    def gather_u(d, c):
        span = pl.ds(marks[c], marks[c + 1] - marks[c])
        if d:
            u_copies[d, 0, c].wait_recv()
        if d + 1 < ny:
            u_copies[d + 1, 0, c] = push(
                ubuf.at[d, 0, span], ubuf.at[d + 1, 0, span], u_send.at[d, 0, c], u_recv.at[d + 1, 0, c], y_next
            )
        u_copies[d, 1, c] = push(
            ubuf.at[d, 0, span], ubuf.at[d, 1, span], u_send.at[d, 1, c], u_recv.at[d, 1, c], core_peer
        )

    for c in range(chunks):
        loads[c].wait()
        if c + 1 == chunks:
            green_load.start()
        prod = jnp.dot(data_v[c], wf[...], preferred_element_type=F32)
        prod = jnp.where(keep, prod.reshape(rows // here, here, wide), 0.0).reshape(rows, wide).astype(BF16)
        sums = jnp.dot(add_rows, prod, preferred_element_type=F32)
        for g in range(groups):
            spec_f[g, c * sensors_chunk:(c + 1) * sensors_chunk, :] = sums[g * stack:g * stack + sensors_chunk]
        lo, hi = marks[c], marks[c + 1]
        for g in range(groups):
            ubuf[0, 0, lo:hi, g * lanes:(g + 1) * lanes] = spec_f[g, lo:hi, :][:, :lanes].astype(BF16)
        if c == 0:
            pl.semaphore_wait(barrier, n_sens + n_par - 2)
        gather_u(0, c)
    c_copies = [push(coef.at[0], coef.at[e], c_send.at[e], c_recv.at[e], par_peer(e)) for e in range(1, n_par)]

    green_s[:, spad - 16:, :] = jnp.zeros((green_s.shape[0], 16, green_s.shape[2]), BF16)

    def split(block):
        green_f[...] = green_v[block].astype(F32)
        for k in range(kper):
            for c in range(2):
                piece = green_f[pl.ds(k * 2 * sensors + c, sensors, stride=2), :]
                green_s[block * kper + k, :sensors, c * width:(c + 1) * width] = piece.astype(BF16)

    steps = [(0, 0)]
    for d in range(1, nz):
        steps += [(d, 0), (d - 1, 1)]
    steps.append((nz - 1, 1))

    def owner(step):
        d, xi = step
        other = xpos if xi == 0 else 1 - xpos
        return ring_member((zring - d + nz) % nz, nz) * 2 + other

    ready = 0
    green_load.wait()
    for d in range(1, ny):
        for c in range(chunks):
            gather_u(d, c)
            if c + 1 < chunks:
                split(owner(steps[ready]))
                ready += 1

    column = jnp.transpose(jnp.broadcast_to(order[...].astype(F32), (128, sensors)))[:, :1]
    wanted = jnp.broadcast_to(column, (sensors, spad))
    picked = jnp.zeros((sensors, groups * lanes), F32)
    position = iota((sensors, spad), 1)
    for d in range(ny):
        for ci in range(2):
            if ci:
                for c in range(chunks):
                    u_copies[d, 1, c].wait_recv()
            source = ring_member((yring - d + ny) % ny, ny) * 2 + (cpos if ci == 0 else 1 - cpos)
            match = (wanted == (position + source * sensors).astype(F32)) & (position < sensors)
            picked = picked + jnp.dot(match.astype(F32).astype(BF16), ubuf[d, ci], preferred_element_type=F32)
    vbuf[0, 0, spad - 16:, :] = jnp.zeros((16, groups * lanes), BF16)
    vbuf[0, 0, :sensors, :] = picked.astype(BF16)

    partner = {"par": (b // 2) * 2 + (1 - xpos)}
    z_next = {"par": ring_member((zring + 1) % nz, nz) * 2 + xpos}
    cut = round_up(spad // 2, 16) if nz > 2 else spad
    z_copies = {}
    x_copies = {}

    halves = [pl.ds(0, cut)] + ([pl.ds(cut, spad - cut)] if cut < spad else [])

    def gather_v(d):
        for p, span in enumerate(halves):
            if d:
                z_copies[d, p].wait_recv()
            if d + 1 < nz:
                z_copies[d + 1, p] = push(
                    vbuf.at[d, 0, span], vbuf.at[d + 1, 0, span], z_send.at[d, p], z_recv.at[d + 1, p], z_next
                )
            if d + 1 < nz or p == 0:
                x_copies[d, p] = push(
                    vbuf.at[d, 0, span], vbuf.at[d, 1, span], x_send.at[d, p], x_recv.at[d, p], partner
                )

    gather_v(0)
    freq_pair = iota((nfreq, 2 * nfreq), 0) == iota((nfreq, 2 * nfreq), 1) // 2
    wi = table(freq_rows, freq_pair.astype(F32).astype(BF16), iota((1, 2 * nfreq), 1) % 2, nt, nfreq)
    steps_here = wi_out.shape[1]
    for p in range(wi_out.shape[0]):
        wi_out[p] = wi[p * steps_here:(p + 1) * steps_here]

    rs_copies = {}
    a_copies = []

    def products(index):
        d, xi = steps[index]
        if xi:
            for p, span in enumerate(halves):
                if (d, p) in x_copies:
                    x_copies[d, p].wait_recv()
                if d + 2 == nz and p == 1:
                    z_copies[nz, 1] = push(
                        vbuf.at[d, 1, span], vbuf.at[d + 1, 1, span], z_send.at[nz, 1], z_recv.at[nz, 1], z_next
                    )
                if d + 1 == nz and p == 1:
                    z_copies[nz, 1].wait_recv()
        elif d:
            gather_v(d)
        block = owner(steps[index])
        vt[...] = jnp.transpose(vbuf[d, xi])
        pair = 2 * here
        for k in range(kper):
            left = jnp.concatenate(
                [vt[g * lanes + k * pair:g * lanes + (k + 1) * pair, :] for g in range(groups)], axis=0
            )
            prod = jnp.dot(left, green_s[block * kper + k], preferred_element_type=F32)
            for g in range(groups):
                real = prod[g * pair:g * pair + here]
                imag = prod[g * pair + here:(g + 1) * pair]
                re = real[:, :width] + imag[:, width:]
                im = imag[:, :width] - real[:, width:]
                part[index, g, k * pair:(k + 1) * pair, :] = jnp.concatenate([re, im], axis=0).astype(BF16)
        rs_copies[index] = [
            push(
                part.at[index, (a + e) % n_sens], rsbuf.at[index, e - 1],
                rs_send.at[index, e - 1], rs_recv.at[index, e - 1], sens_peer(e),
            )
            for e in range(1, n_sens)
        ]

    def reduce(index):
        for copy in rs_copies[index]:
            copy.wait_recv()
        total = part[index, a].astype(F32)
        for e in range(1, n_sens):
            total = total + rsbuf[index, e - 1].astype(F32)
        if index == 0:
            gin[b] = total.astype(BF16)
        else:
            adj[index] = total.astype(BF16)
            a_copies.append(
                push(adj.at[index], gin.at[b], a_send.at[index], a_recv.at[index], {"par": owner(steps[index])})
            )

    for index in range(n_par):
        if index >= ready:
            split(owner(steps[index]))
        products(index)
        if index >= 2:
            reduce(index - 2)
    reduce(n_par - 2)
    reduce(n_par - 1)

    for copy in c_copies:
        copy.wait_recv()
    kap = coef[0, 0]
    tht = coef[0, 1]
    for e in range(1, n_par):
        kap = kap + coef[e, 0]
        tht = tht + coef[e, 1]
    lane = iota((n_par, width), 1)
    sub = iota((n_par, width), 0)
    first_row = lane < cg
    last_row = lane >= width - cg
    first_col = (sub == 0) & (lane % cg == 0)
    last_col = (sub == n_par - 1) & (lane % cg == cg - 1)
    up = pltpu.roll(tht, cg, 1)
    down = pltpu.roll(tht, width - cg, 1)
    left_of = jnp.concatenate([pltpu.roll(tht, 1, 1)[n_par - 1:], tht[:n_par - 1]], axis=0)
    right_of = jnp.concatenate([tht[1:], pltpu.roll(tht, width - 1, 1)[:1]], axis=0)
    north = 0.5 * (tht + jnp.where(first_row, tht, up))
    south = 0.5 * (tht + jnp.where(last_row, tht, down))
    west = 0.5 * (tht + jnp.where(first_col, tht, left_of))
    east = 0.5 * (tht + jnp.where(last_col, tht, right_of))
    diagonal = kap + north + south + west + east
    north = jnp.where(first_row, 0.0, north)
    south = jnp.where(last_row, 0.0, south)
    west = jnp.where(first_col, 0.0, west)
    east = jnp.where(last_col, 0.0, east)
    for index, value in enumerate((diagonal, north, south, west, east)):
        sf[index * n_par:(index + 1) * n_par, :] = value

    for copy in a_copies:
        copy.wait_recv()
    alphas, betas = chebyshev_scalars()
    tile = 16
    low = 8

    def row(index, block):
        return jnp.broadcast_to(sf[index * n_par + block:index * n_par + block + 1, :], (low, width))

    def smooth(chunk, carry):
        start = pl.multiple_of(chunk * tile, tile)
        loaded = [gin[q, pl.ds(start, tile), :].astype(F32) for q in range(n_par)]
        place = iota((low, width), 1) // cg
        rows_out = []
        for part_index in range(tile // low):
            res = [v[part_index * low:(part_index + 1) * low] for v in loaded]
            dirn = res
            x = [alphas[0] * v for v in res]
            for sweep in range(1, SWEEPS):
                wrap_left = pltpu.roll(dirn[n_par - 1], 1, 1)
                wrap_right = pltpu.roll(dirn[0], width - 1, 1)
                fresh = []
                for q in range(n_par):
                    u = dirn[q]
                    w = dirn[q - 1] if q else wrap_left
                    e = dirn[q + 1] if q + 1 < n_par else wrap_right
                    value = (
                        row(0, q) * u
                        - row(1, q) * pltpu.roll(u, cg, 1)
                        - row(2, q) * pltpu.roll(u, width - cg, 1)
                        - row(3, q) * w
                        - row(4, q) * e
                    )
                    fresh.append(res[q] - alphas[sweep - 1] * value)
                res = fresh
                dirn = [r + betas[sweep] * v for r, v in zip(res, dirn)]
                x = [v + alphas[sweep] * u for v, u in zip(x, dirn)]
            moved_rows = []
            for i in range(n_par):
                value = x[i]
                for q in range(n_par):
                    if q != i:
                        value = jnp.where(place == q, pltpu.roll(x[q], ((q - i) % n_par) * cg, 1), value)
                moved_rows.append(value)
            rows_out.append(moved_rows)
        for i in range(n_par):
            both = jnp.concatenate([piece[i] for piece in rows_out], axis=0)
            ysend[i, pl.ds(start, tile), :] = both.astype(BF16)
        return carry

    parts = y_send.shape[0]
    cuts = [fields // tile * i // parts for i in range(parts + 1)]
    y_copies = []
    for half in range(parts):
        lax.fori_loop(cuts[half], cuts[half + 1], smooth, 0)
        span = pl.ds(cuts[half] * tile, (cuts[half + 1] - cuts[half]) * tile)
        for e in range(1, n_par):
            target = (b + e) % n_par
            y_copies.append(
                push(
                    ysend.at[target, span], sin.at[b, span],
                    y_send.at[half, e], y_recv.at[half, e], {"par": target},
                )
            )
    sin[b] = ysend[b]
    for copy in y_copies:
        copy.wait_recv()
    out[...] = sin[...]
    for copy in sends:
        copy.wait_send()


def inverse_kernel(n_par, here, smoothed, wi, out, sf, ordered, tall):
    width = out.shape[1]
    cg = width // n_par
    fields = smoothed.shape[0]

    @pl.when(pl.program_id(0) == 0)
    def _():
        source = iota((width, 1), 0)
        target = source % cg * n_par + source // cg
        perm = jnp.broadcast_to(target, (width, width)) == iota((width, width), 1)
        sf[...] = jnp.dot(smoothed[...], perm.astype(F32).astype(BF16), preferred_element_type=F32)
        for r in range(here):
            ordered[r] = sf[pl.ds(r, fields // here, stride=here), :].astype(BF16)

    steps = tall.shape[0] // here
    for r in range(here):
        tall[pl.ds(r, steps, stride=here), :] = jnp.dot(wi[0], ordered[r], preferred_element_type=F32)
    out[...] = tall[...].astype(BF16)


def local(n_sens, n_par, data, green, freqs, sensor_order, kappa, theta):
    probes, sensors, nt = data.shape
    nfreq, _, _, cells = green.shape
    width = kappa.shape[1]
    kper = nfreq // n_par
    here = probes // n_sens
    lanes = here * 2 * kper
    fields = kper * 2 * here
    spad = round_up(sensors, 16)
    wide = round_up(lanes, 128)
    chunks = 3
    pieces = 3
    flat = jnp.transpose(data, (1, 0, 2)).reshape(chunks, sensors * probes // chunks, nt)
    blocks = green.reshape(n_par, kper * sensors * 2, cells)
    vmem = pl.BlockSpec(memory_space=pltpu.VMEM)
    anywhere = pl.BlockSpec(memory_space=pl.ANY)
    dma = pltpu.SemaphoreType.DMA
    nz = n_par // 2
    block = 2 * kper * here
    smoothed, wi = pl.pallas_call(
        functools.partial(kernel, n_sens, n_par, probes, sensors, kper),
        out_shape=[
            jax.ShapeDtypeStruct((n_par, fields, width), BF16),
            jax.ShapeDtypeStruct((pieces, nt // pieces, 2 * nfreq), BF16),
        ],
        in_specs=[anywhere, anywhere] + [vmem] * 4,
        out_specs=[vmem, vmem],
        scratch_shapes=[
            pltpu.VMEM((nt, wide), BF16),
            pltpu.VMEM(flat.shape, BF16),
            pltpu.VMEM(blocks.shape, BF16),
            pltpu.VMEM(blocks.shape[1:], F32),
            pltpu.VMEM((nfreq, spad, 2 * cells), BF16),
            pltpu.VMEM((n_sens, spad, wide), F32),
            pltpu.VMEM((n_sens // 2, 2, spad, n_sens * lanes), BF16),
            pltpu.VMEM((nz, 2, spad, n_sens * lanes), BF16),
            pltpu.VMEM((n_sens * lanes, spad), BF16),
            pltpu.VMEM((n_par, n_sens, block, cells), BF16),
            pltpu.VMEM((n_par, n_sens - 1, block, cells), BF16),
            pltpu.VMEM((n_par, block, cells), BF16),
            pltpu.VMEM((n_par, block, cells), BF16),
            pltpu.VMEM((n_par, 2, n_par, width), F32),
            pltpu.VMEM((n_par, block, width), BF16),
            pltpu.VMEM((n_par, block, width), BF16),
            pltpu.VMEM((n_par * block, width), F32),
            dma((chunks + 1,)),
            dma((n_sens // 2, 2, chunks)), dma((n_sens // 2, 2, chunks)),
            dma((nz + 1, 2)), dma((nz + 1, 2)),
            dma((nz, 2)), dma((nz, 2)),
            dma((n_par, n_sens - 1)), dma((n_par, n_sens - 1)),
            dma((n_par,)), dma((n_par,)),
            dma((n_par,)), dma((n_par,)),
            dma((min(4, block // 16), n_par)), dma((min(4, block // 16), n_par)),
        ],
        compiler_params=pltpu.CompilerParams(
            collective_id=0, has_side_effects=True, vmem_limit_bytes=56 * 1024 * 1024
        ),
    )(flat, blocks, freqs.reshape(1, nfreq), sensor_order.reshape(1, sensors), kappa, theta)
    total = n_par * fields
    out = pl.pallas_call(
        functools.partial(inverse_kernel, n_par, here),
        out_shape=jax.ShapeDtypeStruct((nt * here, width), BF16),
        grid=(pieces,),
        in_specs=[
            pl.BlockSpec((total, width), lambda i: (0, 0)),
            pl.BlockSpec((1, nt // pieces, 2 * nfreq), lambda i: (i, 0, 0)),
        ],
        out_specs=pl.BlockSpec((nt * here // pieces, width), lambda i: (i, 0)),
        scratch_shapes=[
            pltpu.VMEM((total, width), F32),
            pltpu.VMEM((here, total // here, width), BF16),
            pltpu.VMEM((nt * here // pieces, width), F32),
        ],
    )(smoothed.reshape(total, width), wi)
    return jnp.transpose(out.reshape(nt, here, 1, width), (1, 0, 2, 3))


def solution(mesh):
    placed = (
        P(None, "sens", None),
        P(None, "sens", None, "par"),
        P(),
        P("sens"),
        P("par", None),
        P("par", None),
    )
    return jax.shard_map(
        functools.partial(local, mesh.shape["sens"], mesh.shape["par"]),
        mesh=mesh, in_specs=placed, out_specs=P("sens", None, "par", None), check_vma=False,
    )
```

```python
import functools
import math

import jax
import jax.numpy as jnp
from jax import lax
from jax.experimental import pallas as pl
from jax.experimental.pallas import tpu as pltpu
from jax.sharding import PartitionSpec as P

SWEEPS = 6
lower_bound = 0.05
upper_bound = 16.5
MESH = pl.DeviceIdType.MESH
F32 = jnp.float32
BF16 = jnp.bfloat16


def chebyshev_scalars():
    center = 0.5 * (upper_bound + lower_bound)
    radius = 0.5 * (upper_bound - lower_bound)
    alphas = []
    betas = []
    alpha = 1.0 / center
    for sweep_index in range(SWEEPS):
        if sweep_index == 0:
            alpha = 1.0 / center
            beta = 0.0
        else:
            if sweep_index == 1:
                beta = 0.5 * (radius * alpha) ** 2
            else:
                beta = (radius * alpha / 2.0) ** 2
            alpha = 1.0 / (center - beta / alpha)
        alphas.append(alpha)
        betas.append(beta)
    return (alphas, betas)


def iota(shape, dim):
    return lax.broadcasted_iota(jnp.int32, shape, dim)


def round_up(value, unit):
    return -(-value // unit) * unit


def ring_place(z, size):
    odd = z % 2
    return odd * ((z + 1) // 2) + (1 - odd) * ((size - z // 2) % size)


def ring_member(place, size):
    back = ((place + size - 1) % size) // max(size // 2, 1)
    return (1 - back) * (2 * place - 1) + back * (2 * ((size - place) % size))


def table(freqs, chosen, quarter, nt, scale):
    lanes_freq = jnp.dot(freqs, chosen, preferred_element_type=F32)[:1]
    shape = (nt, chosen.shape[1])
    turn = iota(shape, 0).astype(F32) * lanes_freq + quarter.astype(F32) * (nt // 4)
    turn = turn - nt * jnp.floor((turn + 0.5) * (1.0 / nt))
    arc = (nt // 4 - jnp.abs(turn - nt // 2)) * (2.0 * math.pi / nt)
    square = arc * arc
    sine = jnp.full(shape, 1.0 / math.factorial(13), F32)
    for power in (11, 9, 7, 5, 3, 1):
        sign = -1.0 if power % 4 == 3 else 1.0
        sine = sine * square + sign / math.factorial(power)
    return (sine * arc * (-1.0 / math.sqrt(scale))).astype(BF16)


def kernel(
    n_sens, n_par, probes, sensors, kper,
    data_hbm, green_hbm, freqs, order, kappa, theta,
    out, wi_out,
    wf, data_v, green_v, green_f, green_s, spec_f, ubuf, vbuf, vt, part, rsbuf, adj, gin,
    coef, ysend, sin, sf,
    load_sem, u_send, u_recv, z_send, z_recv, x_send, x_recv, rs_send, rs_recv,
    a_send, a_recv, c_send, c_recv, y_send, y_recv,
):
    a = lax.axis_index("sens")
    b = lax.axis_index("par")
    nz = n_par // 2
    xpos = b % 2
    zring = ring_place(b // 2, nz)
    here = probes // n_sens
    lanes = here * 2 * kper
    fields = kper * 2 * here
    spad = ubuf.shape[2]
    groups = n_sens
    width = out.shape[-1]
    cg = width // n_par

    def sens_peer(e):
        return {"sens": (a + e) % n_sens}

    def par_peer(e):
        return {"par": (b + e) % n_par}

    barrier = pltpu.get_barrier_semaphore()
    for e in range(1, n_sens):
        pl.semaphore_signal(barrier, inc=1, device_id=sens_peer(e), device_id_type=MESH)
    for e in range(1, n_par):
        pl.semaphore_signal(barrier, inc=1, device_id=par_peer(e), device_id_type=MESH)

    chunks = data_v.shape[0]
    loads = []
    for c in range(chunks):
        load = pltpu.make_async_copy(data_hbm.at[c], data_v.at[c], load_sem.at[c])
        load.start()
        loads.append(load)
    green_load = pltpu.make_async_copy(green_hbm, green_v, load_sem.at[chunks])

    nt = wf.shape[0]
    nfreq = freqs.shape[1]
    freq_rows = jnp.broadcast_to(freqs[...], (8, nfreq)).astype(F32).astype(BF16)
    wide = wf.shape[1]
    chosen = iota((nfreq, wide), 0) == b * kper + iota((nfreq, wide), 1) // (2 * here)
    wf[...] = table(freq_rows, chosen.astype(F32).astype(BF16), iota((1, wide), 1) // here % 2, nt, nt)

    pick = (iota((width, width), 0) // n_par + b * cg == iota((width, width), 1)).astype(F32)
    own = iota((n_par, width), 1) % n_par == iota((n_par, width), 0)
    for index, ref in enumerate((kappa, theta)):
        spread = jnp.where(own, jnp.broadcast_to(ref[...], (n_par, width)), 0.0)
        coef[0, index] = jnp.dot(spread, pick, precision=lax.Precision.HIGHEST, preferred_element_type=F32)

    rows = data_v.shape[1]
    sensors_chunk = sensors // chunks
    stack = round_up(sensors_chunk, 8)
    pile = groups * stack
    place = iota((pile, 1), 0)
    place = place % stack * groups + place // stack
    group_of = iota((1, rows), 1) // here
    add_rows = jnp.broadcast_to(place, (pile, rows)) == jnp.broadcast_to(group_of, (pile, rows))
    add_rows = add_rows.astype(F32).astype(BF16)
    lane = iota((1, here, wide), 2)
    keep = (lane % here == iota((1, here, wide), 1)) & (lane < lanes)
    marks = [(c * sensors_chunk) // 16 * 16 for c in range(chunks)] + [spad]
    spec_f[:, spad - 16:, :] = jnp.zeros((groups, 16, wide), F32)
    sends = []

    def push(src, dst, ssem, rsem, peer):
        copy = pltpu.make_async_remote_copy(
            src_ref=src, dst_ref=dst, send_sem=ssem, recv_sem=rsem, device_id=peer, device_id_type=MESH
        )
        copy.start()
        sends.append(copy)
        return copy

    ny = n_sens // 2
    cpos = a % 2
    yring = ring_place(a // 2, ny)
    core_peer = {"sens": (a // 2) * 2 + (1 - cpos)}
    y_next = {"sens": ring_member((yring + 1) % ny, ny) * 2 + cpos}
    u_copies = {}

    def gather_u(d, c):
        span = pl.ds(marks[c], marks[c + 1] - marks[c])
        if d:
            u_copies[d, 0, c].wait_recv()
        if d + 1 < ny:
            u_copies[d + 1, 0, c] = push(
                ubuf.at[d, 0, span], ubuf.at[d + 1, 0, span], u_send.at[d, 0, c], u_recv.at[d + 1, 0, c], y_next
            )
        u_copies[d, 1, c] = push(
            ubuf.at[d, 0, span], ubuf.at[d, 1, span], u_send.at[d, 1, c], u_recv.at[d, 1, c], core_peer
        )

    for c in range(chunks):
        loads[c].wait()
        if c + 1 == chunks:
            green_load.start()
        prod = jnp.dot(data_v[c], wf[...], preferred_element_type=F32)
        prod = jnp.where(keep, prod.reshape(rows // here, here, wide), 0.0).reshape(rows, wide).astype(BF16)
        sums = jnp.dot(add_rows, prod, preferred_element_type=F32)
        for g in range(groups):
            spec_f[g, c * sensors_chunk:(c + 1) * sensors_chunk, :] = sums[g * stack:g * stack + sensors_chunk]
        lo, hi = marks[c], marks[c + 1]
        for g in range(groups):
            ubuf[0, 0, lo:hi, g * lanes:(g + 1) * lanes] = spec_f[g, lo:hi, :][:, :lanes].astype(BF16)
        if c == 0:
            pl.semaphore_wait(barrier, n_sens + n_par - 2)
        gather_u(0, c)
    c_copies = [push(coef.at[0], coef.at[e], c_send.at[e], c_recv.at[e], par_peer(e)) for e in range(1, n_par)]

    green_s[:, spad - 16:, :] = jnp.zeros((green_s.shape[0], 16, green_s.shape[2]), BF16)

    def split(block):
        green_f[...] = green_v[block].astype(F32)
        for k in range(kper):
            for c in range(2):
                piece = green_f[pl.ds(k * 2 * sensors + c, sensors, stride=2), :]
                green_s[block * kper + k, :sensors, c * width:(c + 1) * width] = piece.astype(BF16)

    steps = [(0, 0)]
    for d in range(1, nz):
        steps += [(d, 0), (d - 1, 1)]
    steps.append((nz - 1, 1))

    def owner(step):
        d, xi = step
        other = xpos if xi == 0 else 1 - xpos
        return ring_member((zring - d + nz) % nz, nz) * 2 + other

    ready = 0
    green_load.wait()
    for d in range(1, ny):
        for c in range(chunks):
            gather_u(d, c)
            if c + 1 < chunks:
                split(owner(steps[ready]))
                ready += 1

    column = jnp.transpose(jnp.broadcast_to(order[...].astype(F32), (128, sensors)))[:, :1]
    wanted = jnp.broadcast_to(column, (sensors, spad))
    picked = jnp.zeros((sensors, groups * lanes), F32)
    position = iota((sensors, spad), 1)
    for d in range(ny):
        for ci in range(2):
            if ci:
                for c in range(chunks):
                    u_copies[d, 1, c].wait_recv()
            source = ring_member((yring - d + ny) % ny, ny) * 2 + (cpos if ci == 0 else 1 - cpos)
            match = (wanted == (position + source * sensors).astype(F32)) & (position < sensors)
            picked = picked + jnp.dot(match.astype(F32).astype(BF16), ubuf[d, ci], preferred_element_type=F32)
    vbuf[0, 0, spad - 16:, :] = jnp.zeros((16, groups * lanes), BF16)
    vbuf[0, 0, :sensors, :] = picked.astype(BF16)

    partner = {"par": (b // 2) * 2 + (1 - xpos)}
    z_next = {"par": ring_member((zring + 1) % nz, nz) * 2 + xpos}
    cut = round_up(spad // 2, 16) if nz > 2 else spad
    z_copies = {}
    x_copies = {}

    halves = [pl.ds(0, cut)] + ([pl.ds(cut, spad - cut)] if cut < spad else [])

    def gather_v(d):
        for p, span in enumerate(halves):
            if d:
                z_copies[d, p].wait_recv()
            if d + 1 < nz:
                z_copies[d + 1, p] = push(
                    vbuf.at[d, 0, span], vbuf.at[d + 1, 0, span], z_send.at[d, p], z_recv.at[d + 1, p], z_next
                )
            if d + 1 < nz or p == 0:
                x_copies[d, p] = push(
                    vbuf.at[d, 0, span], vbuf.at[d, 1, span], x_send.at[d, p], x_recv.at[d, p], partner
                )

    gather_v(0)
    freq_pair = iota((nfreq, 2 * nfreq), 0) == iota((nfreq, 2 * nfreq), 1) // 2
    wi = table(freq_rows, freq_pair.astype(F32).astype(BF16), iota((1, 2 * nfreq), 1) % 2, nt, nfreq)
    steps_here = wi_out.shape[1]
    for p in range(wi_out.shape[0]):
        wi_out[p] = wi[p * steps_here:(p + 1) * steps_here]

    rs_copies = {}
    a_copies = []

    def products(index):
        d, xi = steps[index]
        if xi:
            for p, span in enumerate(halves):
                if (d, p) in x_copies:
                    x_copies[d, p].wait_recv()
                if d + 2 == nz and p == 1:
                    z_copies[nz, 1] = push(
                        vbuf.at[d, 1, span], vbuf.at[d + 1, 1, span], z_send.at[nz, 1], z_recv.at[nz, 1], z_next
                    )
                if d + 1 == nz and p == 1:
                    z_copies[nz, 1].wait_recv()
        elif d:
            gather_v(d)
        block = owner(steps[index])
        vt[...] = jnp.transpose(vbuf[d, xi])
        pair = 2 * here
        for k in range(kper):
            left = jnp.concatenate(
                [vt[g * lanes + k * pair:g * lanes + (k + 1) * pair, :] for g in range(groups)], axis=0
            )
            prod = jnp.dot(left, green_s[block * kper + k], preferred_element_type=F32)
            for g in range(groups):
                real = prod[g * pair:g * pair + here]
                imag = prod[g * pair + here:(g + 1) * pair]
                re = real[:, :width] + imag[:, width:]
                im = imag[:, :width] - real[:, width:]
                part[index, g, k * pair:(k + 1) * pair, :] = jnp.concatenate([re, im], axis=0).astype(BF16)
        rs_copies[index] = [
            push(
                part.at[index, (a + e) % n_sens], rsbuf.at[index, e - 1],
                rs_send.at[index, e - 1], rs_recv.at[index, e - 1], sens_peer(e),
            )
            for e in range(1, n_sens)
        ]

    def reduce(index):
        for copy in rs_copies[index]:
            copy.wait_recv()
        total = part[index, a].astype(F32)
        for e in range(1, n_sens):
            total = total + rsbuf[index, e - 1].astype(F32)
        if index == 0:
            gin[b] = total.astype(BF16)
        else:
            adj[index] = total.astype(BF16)
            a_copies.append(
                push(adj.at[index], gin.at[b], a_send.at[index], a_recv.at[index], {"par": owner(steps[index])})
            )

    for index in range(n_par):
        if index >= ready:
            split(owner(steps[index]))
        products(index)
        if index >= 2:
            reduce(index - 2)
    reduce(n_par - 2)
    reduce(n_par - 1)

    for copy in c_copies:
        copy.wait_recv()
    kap = coef[0, 0]
    tht = coef[0, 1]
    for e in range(1, n_par):
        kap = kap + coef[e, 0]
        tht = tht + coef[e, 1]
    lane = iota((n_par, width), 1)
    sub = iota((n_par, width), 0)
    first_row = lane < cg
    last_row = lane >= width - cg
    first_col = (sub == 0) & (lane % cg == 0)
    last_col = (sub == n_par - 1) & (lane % cg == cg - 1)
    up = pltpu.roll(tht, cg, 1)
    down = pltpu.roll(tht, width - cg, 1)
    left_of = jnp.concatenate([pltpu.roll(tht, 1, 1)[n_par - 1:], tht[:n_par - 1]], axis=0)
    right_of = jnp.concatenate([tht[1:], pltpu.roll(tht, width - 1, 1)[:1]], axis=0)
    north = 0.5 * (tht + jnp.where(first_row, tht, up))
    south = 0.5 * (tht + jnp.where(last_row, tht, down))
    west = 0.5 * (tht + jnp.where(first_col, tht, left_of))
    east = 0.5 * (tht + jnp.where(last_col, tht, right_of))
    diagonal = kap + north + south + west + east
    north = jnp.where(first_row, 0.0, north)
    south = jnp.where(last_row, 0.0, south)
    west = jnp.where(first_col, 0.0, west)
    east = jnp.where(last_col, 0.0, east)
    for index, value in enumerate((diagonal, north, south, west, east)):
        sf[index * n_par:(index + 1) * n_par, :] = value

    for copy in a_copies:
        copy.wait_recv()
    alphas, betas = chebyshev_scalars()
    tile = 16
    low = 8

    def row(index, block):
        return jnp.broadcast_to(sf[index * n_par + block:index * n_par + block + 1, :], (low, width))

    def smooth(chunk, carry):
        start = pl.multiple_of(chunk * tile, tile)
        loaded = [gin[q, pl.ds(start, tile), :].astype(F32) for q in range(n_par)]
        place = iota((low, width), 1) // cg
        rows_out = []
        for part_index in range(tile // low):
            res = [v[part_index * low:(part_index + 1) * low] for v in loaded]
            dirn = res
            x = [alphas[0] * v for v in res]
            for sweep in range(1, SWEEPS):
                wrap_left = pltpu.roll(dirn[n_par - 1], 1, 1)
                wrap_right = pltpu.roll(dirn[0], width - 1, 1)
                fresh = []
                for q in range(n_par):
                    u = dirn[q]
                    w = dirn[q - 1] if q else wrap_left
                    e = dirn[q + 1] if q + 1 < n_par else wrap_right
                    value = (
                        row(0, q) * u
                        - row(1, q) * pltpu.roll(u, cg, 1)
                        - row(2, q) * pltpu.roll(u, width - cg, 1)
                        - row(3, q) * w
                        - row(4, q) * e
                    )
                    fresh.append(res[q] - alphas[sweep - 1] * value)
                res = fresh
                dirn = [r + betas[sweep] * v for r, v in zip(res, dirn)]
                x = [v + alphas[sweep] * u for v, u in zip(x, dirn)]
            moved_rows = []
            for i in range(n_par):
                value = x[i]
                for q in range(n_par):
                    if q != i:
                        value = jnp.where(place == q, pltpu.roll(x[q], ((q - i) % n_par) * cg, 1), value)
                moved_rows.append(value)
            rows_out.append(moved_rows)
        for i in range(n_par):
            both = jnp.concatenate([piece[i] for piece in rows_out], axis=0)
            ysend[i, pl.ds(start, tile), :] = both.astype(BF16)
        return carry

    parts = y_send.shape[0]
    cuts = [fields // tile * i // parts for i in range(parts + 1)]
    y_copies = []
    for half in range(parts):
        lax.fori_loop(cuts[half], cuts[half + 1], smooth, 0)
        span = pl.ds(cuts[half] * tile, (cuts[half + 1] - cuts[half]) * tile)
        for e in range(1, n_par):
            target = (b + e) % n_par
            y_copies.append(
                push(
                    ysend.at[target, span], sin.at[b, span],
                    y_send.at[half, e], y_recv.at[half, e], {"par": target},
                )
            )
    sin[b] = ysend[b]
    for copy in y_copies:
        copy.wait_recv()
    out[...] = sin[...]
    for copy in sends:
        copy.wait_send()


def inverse_kernel(n_par, here, smoothed, wi, out, sf, ordered, tall):
    width = out.shape[1]
    cg = width // n_par
    fields = smoothed.shape[0]

    @pl.when(pl.program_id(0) == 0)
    def _():
        source = iota((width, 1), 0)
        target = source % cg * n_par + source // cg
        perm = jnp.broadcast_to(target, (width, width)) == iota((width, width), 1)
        sf[...] = jnp.dot(smoothed[...], perm.astype(F32).astype(BF16), preferred_element_type=F32)
        for r in range(here):
            ordered[r] = sf[pl.ds(r, fields // here, stride=here), :].astype(BF16)

    steps = tall.shape[0] // here
    for r in range(here):
        tall[pl.ds(r, steps, stride=here), :] = jnp.dot(wi[0], ordered[r], preferred_element_type=F32)
    out[...] = tall[...].astype(BF16)


def local(n_sens, n_par, data, green, freqs, sensor_order, kappa, theta):
    probes, sensors, nt = data.shape
    nfreq, _, _, cells = green.shape
    width = kappa.shape[1]
    kper = nfreq // n_par
    here = probes // n_sens
    lanes = here * 2 * kper
    fields = kper * 2 * here
    spad = round_up(sensors, 16)
    wide = round_up(lanes, 128)
    chunks = 3
    pieces = 1
    flat = jnp.transpose(data, (1, 0, 2)).reshape(chunks, sensors * probes // chunks, nt)
    blocks = green.reshape(n_par, kper * sensors * 2, cells)
    vmem = pl.BlockSpec(memory_space=pltpu.VMEM)
    anywhere = pl.BlockSpec(memory_space=pl.ANY)
    dma = pltpu.SemaphoreType.DMA
    nz = n_par // 2
    block = 2 * kper * here
    smoothed, wi = pl.pallas_call(
        functools.partial(kernel, n_sens, n_par, probes, sensors, kper),
        out_shape=[
            jax.ShapeDtypeStruct((n_par, fields, width), BF16),
            jax.ShapeDtypeStruct((pieces, nt // pieces, 2 * nfreq), BF16),
        ],
        in_specs=[anywhere, anywhere] + [vmem] * 4,
        out_specs=[vmem, vmem],
        scratch_shapes=[
            pltpu.VMEM((nt, wide), BF16),
            pltpu.VMEM(flat.shape, BF16),
            pltpu.VMEM(blocks.shape, BF16),
            pltpu.VMEM(blocks.shape[1:], F32),
            pltpu.VMEM((nfreq, spad, 2 * cells), BF16),
            pltpu.VMEM((n_sens, spad, wide), F32),
            pltpu.VMEM((n_sens // 2, 2, spad, n_sens * lanes), BF16),
            pltpu.VMEM((nz, 2, spad, n_sens * lanes), BF16),
            pltpu.VMEM((n_sens * lanes, spad), BF16),
            pltpu.VMEM((n_par, n_sens, block, cells), BF16),
            pltpu.VMEM((n_par, n_sens - 1, block, cells), BF16),
            pltpu.VMEM((n_par, block, cells), BF16),
            pltpu.VMEM((n_par, block, cells), BF16),
            pltpu.VMEM((n_par, 2, n_par, width), F32),
            pltpu.VMEM((n_par, block, width), BF16),
            pltpu.VMEM((n_par, block, width), BF16),
            pltpu.VMEM((n_par * block, width), F32),
            dma((chunks + 1,)),
            dma((n_sens // 2, 2, chunks)), dma((n_sens // 2, 2, chunks)),
            dma((nz + 1, 2)), dma((nz + 1, 2)),
            dma((nz, 2)), dma((nz, 2)),
            dma((n_par, n_sens - 1)), dma((n_par, n_sens - 1)),
            dma((n_par,)), dma((n_par,)),
            dma((n_par,)), dma((n_par,)),
            dma((min(4, block // 16), n_par)), dma((min(4, block // 16), n_par)),
        ],
        compiler_params=pltpu.CompilerParams(
            collective_id=0, has_side_effects=True, vmem_limit_bytes=56 * 1024 * 1024
        ),
    )(flat, blocks, freqs.reshape(1, nfreq), sensor_order.reshape(1, sensors), kappa, theta)
    total = n_par * fields
    out = pl.pallas_call(
        functools.partial(inverse_kernel, n_par, here),
        out_shape=jax.ShapeDtypeStruct((nt * here, width), BF16),
        grid=(pieces,),
        in_specs=[
            pl.BlockSpec((total, width), lambda i: (0, 0)),
            pl.BlockSpec((1, nt // pieces, 2 * nfreq), lambda i: (i, 0, 0)),
        ],
        out_specs=pl.BlockSpec((nt * here // pieces, width), lambda i: (i, 0)),
        scratch_shapes=[
            pltpu.VMEM((total, width), F32),
            pltpu.VMEM((here, total // here, width), BF16),
            pltpu.VMEM((nt * here // pieces, width), F32),
        ],
    )(smoothed.reshape(total, width), wi)
    return jnp.transpose(out.reshape(nt, here, 1, width), (1, 0, 2, 3))


def solution(mesh):
    placed = (
        P(None, "sens", None),
        P(None, "sens", None, "par"),
        P(),
        P("sens"),
        P("par", None),
        P("par", None),
    )
    return jax.shard_map(
        functools.partial(local, mesh.shape["sens"], mesh.shape["par"]),
        mesh=mesh, in_specs=placed, out_specs=P("sens", None, "par", None), check_vma=False,
    )
```
